32 devices in a mesh: dp: 2 (over x), row: 4 (over y, core), col: 4 (over z).
Axes of the slice: x: 2, y: 2, z: 4, core: 2. Of those that a mesh axis runs over, the one named last changes fastest.
Arguments:
- tokens: bfloat16 [512, 8192], P(('dp', 'col'), 'row'), may hold values from -6 to 6
- cotangent: bfloat16 [512, 8192], P(('dp', 'col'), 'row'), may hold values from -6 to 6
- gate_blocks: bfloat16 [4, 4, 336, 128, 128], P('row', 'col'), may hold values from -0.09375 to 0.09375
- gate_index: int32 [4, 4, 336, 2], P('row', 'col'), may hold values from -1 to 27, as said below
- up_blocks: bfloat16 [4, 4, 336, 128, 128], P('row', 'col'), may hold values from -0.09375 to 0.09375
- up_index: int32 [4, 4, 336, 2], P('row', 'col'), may hold values from -1 to 27, as said below
- down_blocks: bfloat16 [4, 4, 336, 128, 128], P('row', 'col'), may hold values from -0.0625 to 0.0625
- down_index: int32 [4, 4, 336, 2], P('row', 'col'), may hold values from -1 to 27, as said below
Outputs:
- output: bfloat16 [512, 8192], P(('dp', 'col'), 'row')
- input_grad: bfloat16 [512, 8192], P(('dp', 'col'), 'row')
- gate_grad: bfloat16 [4, 4, 336, 128, 128], P('row', 'col')
- up_grad: bfloat16 [4, 4, 336, 128, 128], P('row', 'col')
- down_grad: bfloat16 [4, 4, 336, 128, 128], P('row', 'col')
The draws below stay inside these ranges and needn't reach their ends.
Inputs may be any that keep to these rules, and one draw needn't show every extreme that they name: `gate_index`: in each tile the listed slots come first and name distinct positions, with a first entry below 16 and a second below 28; every slot after them holds -1 in both entries. A tile lists 112 to 336 blocks, and some tile lists exactly 336. `up_index`: as for gate_index, with a pattern of its own. `down_index`: as for gate_index with the entries' roles swapped: the first is below 28, the second below 16. A tile lists 112 to 336 blocks, and some tile lists exactly 336.
All inputs are finite; a program needn't handle non-finite values.
Results may differ from the reference program's by a relative error of at most 0.0059.
Values may be sent and summed in bfloat16 or wider, within the bound.
No kernel may reach another device: no remote copies, remote signals or barrier semaphores. Data moves between devices by JAX's collectives and lax.ppermute only.
A program may use at most 256 MiB of HBM per device.

```python
import jax
import jax.numpy as jnp
from jax import lax

D = 8192
FF = 14336
BLK = 128
TOK = 256
TOKENS = 512
DB = 16
FB = 28
SLOTS = 448
CAP = 336
LOW = 112
N_DP = 2
N_ROW = 4
N_COL = 4


def block_list(key, second_per):
    tiles = N_ROW * N_COL
    tile_keys = jax.random.split(key, tiles)
    orders = jax.vmap(lambda each_key: jax.random.permutation(each_key, SLOTS))(tile_keys)[:, :CAP]
    counts = jax.random.randint(jax.random.fold_in(key, 7), (tiles,), LOW, CAP + 1)
    fullest = jax.random.randint(jax.random.fold_in(key, 11), (), 0, tiles)
    counts = jnp.where(jnp.arange(tiles) == fullest, CAP, counts)
    used = jnp.arange(CAP)[None, :] < counts[:, None]
    first = jnp.where(used, orders // second_per, -1)
    second = jnp.where(used, orders % second_per, -1)
    return jnp.stack([first, second], axis=-1).astype(jnp.int32).reshape(N_ROW, N_COL, CAP, 2)


def draw_gate_index(key, part):
    return block_list(jax.random.fold_in(key, 1), FB)


def draw_up_index(key, part):
    return block_list(jax.random.fold_in(key, 2), FB)


def draw_down_index(key, part):
    return block_list(jax.random.fold_in(key, 3), DB)


def shard_levels(own_key, dims, cuts, low, high):
    def one(position, blocks):
        steps = jax.random.uniform(jax.random.fold_in(jax.random.fold_in(own_key, 6), position), (blocks,), jnp.float32, low / len(cuts), high / len(cuts))
        return jnp.repeat(jnp.exp(steps), dims[position] // blocks).reshape((-1,) + (1,) * (len(dims) - position - 1))

    gain = one(*cuts[0])
    for cut in cuts[1:]:
        gain = gain * one(*cut)
    return gain


def noise(rng, dims, deviation, reach, shards=(), kind=jnp.bfloat16):
    loudness = shard_levels(rng, dims, shards, -0.22, 0.18) if shards else 1.0
    result = jax.random.normal(rng, dims, jnp.float32) * deviation * loudness
    return jnp.minimum(jnp.maximum(result, -reach), reach).astype(kind)


def setup_inputs(seed: int = 0) -> dict:
    arg_keys = jax.random.split(jax.random.key(seed), 9)
    return {
        "tokens": noise(arg_keys[0], (TOKENS, D), 1.0, 6.0, ((0, 8), (1, 4))),
        "cotangent": noise(arg_keys[1], (TOKENS, D), 1.0, 6.0, ((0, 8), (1, 4))),
        "gate_blocks": noise(arg_keys[2], (N_ROW, N_COL, CAP, BLK, BLK), (D // 2) ** -0.5, 0.09375, ((0, 4), (1, 4))),
        "gate_index": draw_gate_index(jax.random.fold_in(arg_keys[8], 71), 0),
        "up_blocks": noise(arg_keys[4], (N_ROW, N_COL, CAP, BLK, BLK), (D // 2) ** -0.5, 0.09375, ((0, 4), (1, 4))),
        "up_index": draw_up_index(jax.random.fold_in(arg_keys[8], 71), 0),
        "down_blocks": noise(arg_keys[6], (N_ROW, N_COL, CAP, BLK, BLK), (FF // 2) ** -0.5, 0.0625, ((0, 4), (1, 4))),
        "down_index": draw_down_index(jax.random.fold_in(arg_keys[8], 71), 0),
    }


def tile_positions(index_list, first_per, second_per):
    used = index_list[..., 0] >= 0
    first_at = jnp.arange(index_list.shape[0], dtype=jnp.int32)[:, None, None] * first_per + jnp.maximum(index_list[..., 0], 0).astype(jnp.int32)
    second_at = jnp.arange(index_list.shape[1], dtype=jnp.int32)[None, :, None] * second_per + jnp.maximum(index_list[..., 1], 0).astype(jnp.int32)
    return used, first_at, second_at


def densify(blocks, index_list, first_per, second_per):
    used, first_at, second_at = tile_positions(index_list, first_per, second_per)
    first_total = index_list.shape[0] * first_per
    second_total = index_list.shape[1] * second_per
    values = jnp.where(used[..., None, None], blocks.astype(jnp.float32), jnp.float32(0.0))
    grid = jnp.zeros((first_total, second_total, BLK, BLK), jnp.float32)
    grid = grid.at[first_at, second_at].add(values)
    return grid.transpose(0, 2, 1, 3).reshape(first_total * BLK, second_total * BLK).astype(jnp.bfloat16)


def extract(full, index_list, first_per, second_per):
    used, first_at, second_at = tile_positions(index_list, first_per, second_per)
    shaped = full.reshape(index_list.shape[0] * first_per, BLK, index_list.shape[1] * second_per, BLK)
    picked = shaped[first_at, :, second_at, :]
    return jnp.where(used[..., None, None], picked, jnp.float32(0.0))


def contract_last(left, right):
    return lax.dot_general(left, right, (((1,), (1,)), ((), ())), preferred_element_type=jnp.float32)


def contract_first(left, right):
    return lax.dot_general(left, right, (((0,), (0,)), ((), ())), preferred_element_type=jnp.float32)


def reference(tokens, cotangent, gate_blocks, gate_index, up_blocks, up_index, down_blocks, down_index):
    w_gate = densify(gate_blocks, gate_index, DB, FB)
    w_up = densify(up_blocks, up_index, DB, FB)
    down_swapped = down_index.transpose(1, 0, 2, 3)
    w_down = densify(down_blocks.transpose(1, 0, 2, 3, 4), down_swapped, FB, DB)
    scale = 1.0 / (TOKENS ** 0.5)
    outputs = []
    input_grads = []
    gate_total = jnp.zeros(gate_blocks.shape, jnp.float32)
    up_total = jnp.zeros(up_blocks.shape, jnp.float32)
    down_total = jnp.zeros(down_blocks.shape, jnp.float32)
    for group in range(N_DP):
        inputs = tokens[group * TOK:(group + 1) * TOK]
        cotan = cotangent[group * TOK:(group + 1) * TOK]
        gate = jnp.dot(inputs, w_gate, preferred_element_type=jnp.float32)
        up = jnp.dot(inputs, w_up, preferred_element_type=jnp.float32)
        sigma = jax.nn.sigmoid(gate)
        hidden = (gate * sigma * up).astype(jnp.bfloat16)
        outputs.append(jnp.dot(hidden, w_down, preferred_element_type=jnp.float32).astype(jnp.bfloat16))
        grad_hidden = contract_last(cotan, w_down)
        grad_gate = (grad_hidden * up * sigma * (1.0 + gate * (1.0 - sigma))).astype(jnp.bfloat16)
        grad_up = (grad_hidden * gate * sigma).astype(jnp.bfloat16)
        summed = contract_last(grad_gate, w_gate) + contract_last(grad_up, w_up)
        input_grads.append(summed.astype(jnp.bfloat16))
        part_gate = (extract(contract_first(inputs, grad_gate), gate_index, DB, FB) * scale).astype(jnp.bfloat16)
        part_up = (extract(contract_first(inputs, grad_up), up_index, DB, FB) * scale).astype(jnp.bfloat16)
        part_down = (extract(contract_first(hidden, cotan), down_swapped, FB, DB).transpose(1, 0, 2, 3, 4) * scale).astype(jnp.bfloat16)
        part_gate, part_up, part_down = lax.optimization_barrier((part_gate, part_up, part_down))
        gate_total = gate_total + part_gate.astype(jnp.float32)
        up_total = up_total + part_up.astype(jnp.float32)
        down_total = down_total + part_down.astype(jnp.float32)
    return (jnp.concatenate(outputs, axis=0), jnp.concatenate(input_grads, axis=0),
            gate_total.astype(jnp.bfloat16), up_total.astype(jnp.bfloat16), down_total.astype(jnp.bfloat16))
```

```python
import functools
import math

import jax
import jax.numpy as jnp
from jax import lax
from jax.experimental import pallas as pl
from jax.experimental.pallas import tpu as pltpu
from jax.sharding import PartitionSpec as P

BLK = 128
VMEM_LIMIT = 56 * 1024 * 1024
VM = pltpu.VMEM
SM = pltpu.SMEM


def params():
    return pltpu.CompilerParams(vmem_limit_bytes=VMEM_LIMIT)


def cost(flops, nbytes):
    return pl.CostEstimate(flops=int(flops), bytes_accessed=int(nbytes), transcendentals=0)


def tile_of(size, largest):
    tile = largest
    while size % tile:
        tile //= 2
    return tile


def nat_rows(core, half, rows):
    start = core * rows if half == 0 else (1 - core) * rows
    return pl.ds(pl.multiple_of(start, rows), rows)


def slot_table(index_list, first_count, second_count):
    listing = index_list[0, 0]
    flat = jnp.where(listing[:, 0] >= 0, listing[:, 0] * second_count + listing[:, 1], -1)
    slots = jnp.arange(1, flat.shape[0] + 1, dtype=jnp.int32)
    positions = jnp.arange(first_count * second_count, dtype=jnp.int32)
    hits = flat[None, :] == positions[:, None]
    table = jnp.sum(jnp.where(hits, slots[None, :], 0), axis=1) - 1
    count = jnp.sum((flat >= 0).astype(jnp.int32))
    return table, count.reshape(1)


def densify_kernel(cols, table_ref, blocks_ref, out_ref):
    row = pl.program_id(0)
    for j in range(cols):
        slot = table_ref[row * cols + j]
        block = blocks_ref[jnp.maximum(slot, 0)]
        out_ref[:, j * BLK : (j + 1) * BLK] = jnp.where(slot >= 0, block, jnp.zeros_like(block))


def densify(blocks, table, rows, cols):
    slots = blocks.shape[0]
    return pl.pallas_call(
        functools.partial(densify_kernel, cols),
        out_shape=jax.ShapeDtypeStruct((rows * BLK, cols * BLK), blocks.dtype),
        grid_spec=pltpu.PrefetchScalarGridSpec(
            num_scalar_prefetch=1,
            grid=(rows,),
            in_specs=[
                pl.BlockSpec(
                    (slots, BLK, BLK), lambda i, t: (0, 0, 0), pipeline_mode=pl.Buffered(1)
                )
            ],
            out_specs=pl.BlockSpec((BLK, cols * BLK), lambda i, t: (i, 0)),
        ),
        compiler_params=params(),
        cost_estimate=cost(0, (slots + rows * cols) * BLK * BLK * 2),
    )(table, blocks)


def project_kernel(transposed, core_ref, x_ref, w_ref, mine_ref, other_ref):
    half = x_ref.shape[0] // 2
    dims = (((1,), (1 if transposed else 0,)), ((), ()))
    full = lax.dot_general(x_ref[...], w_ref[...], dims, preferred_element_type=jnp.float32)
    first, second = full[:half], full[half:]
    is_first = core_ref[0] == 0
    mine_ref[...] = jnp.where(is_first, first, second)
    other_ref[...] = jnp.where(is_first, second, first).astype(jnp.bfloat16)


def project(core, x, dense, transposed):
    tokens, depth = x.shape
    width = dense.shape[0] if transposed else dense.shape[1]
    tile = tile_of(width, 512)
    if transposed:
        w_spec = pl.BlockSpec((tile, depth), lambda i, c: (i, 0))
    else:
        w_spec = pl.BlockSpec((depth, tile), lambda i, c: (0, i))
    out_spec = pl.BlockSpec((tokens // 2, tile), lambda i, c: (0, i))
    shape = (tokens // 2, width)
    return pl.pallas_call(
        functools.partial(project_kernel, transposed),
        out_shape=(
            jax.ShapeDtypeStruct(shape, jnp.float32),
            jax.ShapeDtypeStruct(shape, jnp.bfloat16),
        ),
        grid_spec=pltpu.PrefetchScalarGridSpec(
            num_scalar_prefetch=1,
            grid=(width // tile,),
            in_specs=[
                pl.BlockSpec((tokens, depth), lambda i, c: (0, 0), pipeline_mode=pl.Buffered(1)),
                w_spec,
            ],
            out_specs=(out_spec, out_spec),
        ),
        compiler_params=params(),
        cost_estimate=cost(2 * tokens * depth * width, 2 * depth * width),
    )(core, x, dense)


def back_kernel(transposed, pairs, chunks, core_ref, *refs):
    pieces = refs[: 2 * pairs]
    weights = refs[2 * pairs : 3 * pairs]
    outs = refs[3 * pairs :]
    half = pieces[0].shape[0]
    dims = (((1,), (1 if transposed else 0,)), ((), ()))
    total = None
    for p in range(pairs):
        panel = jnp.concatenate([pieces[2 * p][...], pieces[2 * p + 1][...]], axis=0)
        part = lax.dot_general(panel, weights[p][...], dims, preferred_element_type=jnp.float32)
        total = part if total is None else total + part
    is_first = core_ref[0] == 0
    first = jnp.where(is_first, total[:half], total[half:])
    second = jnp.where(is_first, total[half:], total[:half])
    rows = 2 * half // chunks
    for d in range(chunks):
        part, at = (first, d * rows) if d < chunks // 2 else (second, d * rows - half)
        outs[d][...] = part[at : at + rows].astype(outs[d].dtype)


def back(core, operands, chunks, transposed):
    pairs = len(operands)
    half, depth = operands[0][0].shape
    dense = operands[0][2]
    width = dense.shape[0] if transposed else dense.shape[1]
    tile = tile_of(width, 256)
    if transposed:
        w_spec = pl.BlockSpec((tile, depth), lambda i, c: (i, 0))
    else:
        w_spec = pl.BlockSpec((depth, tile), lambda i, c: (0, i))
    piece_spec = pl.BlockSpec((half, depth), lambda i, c: (0, 0), pipeline_mode=pl.Buffered(1))
    rows = 2 * half // chunks
    shapes = tuple(
        jax.ShapeDtypeStruct((rows, width), jnp.bfloat16 if d else jnp.float32)
        for d in range(chunks)
    )
    out_spec = pl.BlockSpec((rows, tile), lambda i, c: (0, i))
    args = [a for mine, other, _ in operands for a in (mine, other)]
    args += [dense for _, _, dense in operands]
    return pl.pallas_call(
        functools.partial(back_kernel, transposed, pairs, chunks),
        out_shape=shapes,
        grid_spec=pltpu.PrefetchScalarGridSpec(
            num_scalar_prefetch=1,
            grid=(width // tile,),
            in_specs=[piece_spec] * (2 * pairs) + [w_spec] * pairs,
            out_specs=(out_spec,) * chunks,
        ),
        compiler_params=params(),
        cost_estimate=cost(4 * half * depth * width * pairs, 2 * depth * width * pairs),
    )(core, *args)


def both_halves(core, ref, columns=slice(None)):
    half = ref.shape[0] // 2
    return [ref[nat_rows(core, h, half), columns] for h in (0, 1)]


def block_grad_kernel(groups, left_whole, scale, cols, table_ref, count_ref, core_ref, *refs):
    core = core_ref[0]
    n_left = groups if left_whole else 2 * groups
    lefts = refs[:n_left]
    rights = refs[n_left : 3 * groups]
    out_ref, store, turned, sem = refs[3 * groups :]
    slots = out_ref.shape[0]
    step = pl.program_id(0)
    height = lefts[0].shape[1]
    width = rights[0].shape[1]
    wide = tile_of(width, 256)
    if left_whole:
        pieces = [piece for ref in lefts for piece in both_halves(core, ref)]
    else:
        pieces = [ref[...] for ref in lefts]
    turned[...] = jnp.concatenate(pieces, axis=0).T
    for b in range(width // wide):
        span = slice(b * wide, (b + 1) * wide)
        if left_whole:
            panel = [ref[:, span] for ref in rights]
        else:
            panel = [piece for ref in rights for piece in both_halves(core, ref, span)]
        full = jnp.dot(
            turned[...], jnp.concatenate(panel, axis=0), preferred_element_type=jnp.float32
        )
        full = (full * scale).astype(jnp.bfloat16)
        for di in range(height // BLK):
            for dj in range(wide // BLK):
                position = (step * (height // BLK) + di) * cols + b * (wide // BLK) + dj
                slot = table_ref[position]
                block = full[di * BLK : (di + 1) * BLK, dj * BLK : (dj + 1) * BLK]
                store[jnp.where(slot < 0, slots, slot)] = block

    @pl.when(step == pl.num_programs(0) - 1)
    def _():
        def clear(slot, carry):
            store[slot] = jnp.zeros((BLK, BLK), jnp.bfloat16)
            return carry

        lax.fori_loop(count_ref[0], slots, clear, 0)
        copy = pltpu.make_async_copy(store.at[pl.ds(0, slots)], out_ref, sem)
        copy.start()
        copy.wait()


def block_grads(core, table, count, lefts, rights, left_whole, slots, scale):
    groups = len(lefts) if left_whole else len(rights)
    tokens = (lefts if left_whole else rights)[0].shape[0] * groups
    length, width = lefts[0].shape[1], rights[0].shape[1]
    tile = tile_of(length, 256)
    left_specs = [pl.BlockSpec((a.shape[0], tile), lambda i, *_: (0, i)) for a in lefts]
    right_specs = [
        pl.BlockSpec(a.shape, lambda i, *_: (0, 0), pipeline_mode=pl.Buffered(1)) for a in rights
    ]
    return pl.pallas_call(
        functools.partial(block_grad_kernel, groups, left_whole, scale, width // BLK),
        out_shape=jax.ShapeDtypeStruct((slots, BLK, BLK), jnp.bfloat16),
        grid_spec=pltpu.PrefetchScalarGridSpec(
            num_scalar_prefetch=3,
            grid=(length // tile,),
            in_specs=left_specs + right_specs,
            out_specs=pl.BlockSpec(memory_space=pl.ANY),
            scratch_shapes=[
                VM((slots + 1, BLK, BLK), jnp.bfloat16),
                VM((tile, tokens), jnp.bfloat16),
                pltpu.SemaphoreType.DMA,
            ],
        ),
        compiler_params=params(),
        cost_estimate=cost(2 * tokens * length * width, slots * BLK * BLK * 2),
    )(table, count, core, *lefts, *rights)


def shift(x, axis, by):
    n = lax.axis_size(axis)
    return lax.ppermute(x, axis, [(i, (i + by) % n) for i in range(n)])


def swap_cores(x):
    n = lax.axis_size("row")
    return lax.ppermute(x, "row", [(i, i ^ 1) for i in range(n)])


def add_up(parts):
    total = parts[0].astype(jnp.float32)
    for part in parts[1:]:
        total = total + part.astype(jnp.float32)
    return total


def gather_chunks(x):
    return jnp.concatenate(
        [x] + [shift(x, "col", d) for d in range(1, lax.axis_size("col"))], axis=0
    )


def scatter_chunks(chunks):
    parts = [chunks[0]] + [shift(chunk, "col", -d) for d, chunk in enumerate(chunks) if d]
    return add_up(parts).astype(jnp.bfloat16)


def row_sum(mine, other):
    pair = add_up([mine, swap_cores(other)])
    sent = pair.astype(jnp.bfloat16)
    n = lax.axis_size("row")
    return add_up([pair] + [shift(sent, "row", 2 * s) for s in range(1, n // 2)])


def other_groups(x):
    return [shift(x, "dp", s) for s in range(1, lax.axis_size("dp"))]


def halves_of_groups(mine, other):
    out = [mine, other]
    for far in other_groups(mine):
        out += [far, swap_cores(far)]
    return out


def on_device(
    tokens, cotangent, gate_blocks, gate_index, up_blocks, up_index, down_blocks, down_index
):
    n_col = lax.axis_size("col")
    core = lax.rem(lax.axis_index("row"), 2).astype(jnp.int32).reshape(1)
    feats = tokens.shape[1] // BLK
    units = 14336 // BLK // n_col
    slots = gate_blocks.shape[2]
    group_rows = tokens.shape[0] * n_col
    scale = 1.0 / math.sqrt(group_rows * lax.axis_size("dp"))

    gate_table, gate_count = slot_table(gate_index, feats, units)
    up_table, up_count = slot_table(up_index, feats, units)
    down_table, down_count = slot_table(down_index, units, feats)

    x_all = gather_chunks(tokens)
    c_all = gather_chunks(cotangent)
    w_gate = densify(gate_blocks[0, 0], gate_table, feats, units)
    w_up = densify(up_blocks[0, 0], up_table, feats, units)
    w_down = densify(down_blocks[0, 0], down_table, units, feats)

    gate = row_sum(*project(core, x_all, w_gate, False))
    up = row_sum(*project(core, x_all, w_up, False))
    grad_hidden = row_sum(*project(core, c_all, w_down, True))
    x_groups = [x_all] + other_groups(x_all)
    c_groups = [c_all] + other_groups(c_all)

    sigma = jax.nn.sigmoid(gate)
    hidden = (gate * sigma * up).astype(jnp.bfloat16)
    grad_gate = (grad_hidden * up * sigma * (1.0 + gate * (1.0 - sigma))).astype(jnp.bfloat16)
    grad_up = (grad_hidden * gate * sigma).astype(jnp.bfloat16)

    hidden_other = swap_cores(hidden)
    output = scatter_chunks(back(core, [(hidden, hidden_other, w_down)], n_col, False))
    gate_other, up_other = swap_cores(grad_gate), swap_cores(grad_up)
    input_grad = scatter_chunks(
        back(
            core,
            [(grad_gate, gate_other, w_gate), (grad_up, up_other, w_up)],
            n_col,
            True,
        )
    )
    down_grad = block_grads(
        core,
        down_table,
        down_count,
        halves_of_groups(hidden, hidden_other),
        c_groups,
        False,
        slots,
        scale,
    )
    gate_grad = block_grads(
        core,
        gate_table,
        gate_count,
        x_groups,
        halves_of_groups(grad_gate, gate_other),
        True,
        slots,
        scale,
    )
    up_grad = block_grads(
        core,
        up_table,
        up_count,
        x_groups,
        halves_of_groups(grad_up, up_other),
        True,
        slots,
        scale,
    )
    shape = gate_blocks.shape
    return (
        output,
        input_grad,
        gate_grad.reshape(shape),
        up_grad.reshape(shape),
        down_grad.reshape(shape),
    )


def solution(mesh):
    return jax.shard_map(
        on_device,
        mesh=mesh,
        in_specs=(
            P(("dp", "col"), "row"),
            P(("dp", "col"), "row"),
            P("row", "col", None, None, None),
            P("row", "col", None, None),
            P("row", "col", None, None, None),
            P("row", "col", None, None),
            P("row", "col", None, None, None),
            P("row", "col", None, None),
        ),
        out_specs=(
            P(("dp", "col"), "row"),
            P(("dp", "col"), "row"),
            P("row", "col", None, None, None),
            P("row", "col", None, None, None),
            P("row", "col", None, None, None),
        ),
        check_vma=False,
    )
```

```python
import functools
import math

import jax
import jax.numpy as jnp
from jax import lax
from jax.experimental import pallas as pl
from jax.experimental.pallas import tpu as pltpu
from jax.sharding import PartitionSpec as P

BLK = 128
AHEAD = 3
COST = 0.000001
MARK = 200000
WIDE = 1792
FF = 14336
VMEM_LIMIT = 56 * 1024 * 1024
VM = pltpu.VMEM
SM = pltpu.SMEM


def params():
    return pltpu.CompilerParams(vmem_limit_bytes=VMEM_LIMIT)


def cost(flops, nbytes):
    return pl.CostEstimate(
        flops=int(flops * COST), bytes_accessed=int(nbytes * COST), transcendentals=0
    )


def tile_of(size, largest):
    return max(t for t in range(BLK, largest + 1, BLK) if size % t == 0)


def rows_at(start, rows):
    return pl.ds(pl.multiple_of(start, rows), rows)


def whole(memory_space):
    return pl.BlockSpec(memory_space=memory_space)


def natural_to_own(core, parts, ref, columns=slice(None)):
    rows = ref.shape[0] // (2 * parts)
    pieces = []
    for p in range(parts):
        pieces.append(ref[rows_at((2 * p + core) * rows, rows), columns])
        pieces.append(ref[rows_at((2 * p + 1 - core) * rows, rows), columns])
    return pieces


def after(x, *earlier):
    return lax.optimization_barrier((x, *earlier))[0]


def slot_table(index_list, first_count, second_count):
    listing = index_list[0, 0]
    slots = listing.shape[0]
    flat = jnp.where(listing[:, 0] >= 0, listing[:, 0] * second_count + listing[:, 1], -1)
    positions = jnp.arange(first_count * second_count, dtype=jnp.int32)
    hits = flat[None, :] == positions[:, None]
    back_from = slots - jnp.arange(slots, dtype=jnp.int32)
    table = slots - jnp.sum(jnp.where(hits, back_from[None, :], 0), axis=1)
    count = jnp.sum((flat >= 0).astype(jnp.int32))
    return table, count.reshape(1)


def densify_kernel(mats, rows, cols, panels, *refs):
    tables, blocks = refs[:mats], refs[mats : 2 * mats]
    outs = refs[-4 - mats : -4]
    store, stage, in_sem, out_sem = refs[-4:]
    slots = blocks[0].shape[0]
    loads = [
        pltpu.make_async_copy(blocks[m], store.at[m, pl.ds(0, slots)], in_sem.at[m])
        for m in range(mats)
    ]
    for load in loads:
        load.start()
    high = rows // panels
    writes = []
    for m in range(mats):
        store[m, slots] = jnp.zeros((BLK, BLK), jnp.bfloat16)
        loads[m].wait()
        for g in range(panels):
            if m:
                writes[(m - 1) * panels + g].wait()

            def fill(r, carry, m=m, g=g):
                for j in range(cols):
                    slot = tables[m][(g * high + r) * cols + j]
                    stage[g, rows_at(r * BLK, BLK), j * BLK : (j + 1) * BLK] = store[m, slot]
                return carry

            lax.fori_loop(0, high, fill, 0)
            write = pltpu.make_async_copy(
                stage.at[g], outs[m].at[pl.ds(g * high * BLK, high * BLK)], out_sem.at[g]
            )
            write.start()
            writes.append(write)
    for write in writes[-panels:]:
        write.wait()


def densify(tables, blocks, rows, cols, *earlier):
    mats = len(blocks)
    slots = blocks[0].shape[0]
    panels = 4 if rows % 4 == 0 else 1
    shape = jax.ShapeDtypeStruct((rows * BLK, cols * BLK), jnp.bfloat16)
    return pl.pallas_call(
        functools.partial(densify_kernel, mats, rows, cols, panels),
        out_shape=(shape,) * mats,
        in_specs=[whole(SM)] * mats + [whole(pl.ANY)] * (mats + len(earlier)),
        out_specs=(whole(pl.ANY),) * mats,
        scratch_shapes=[
            VM((mats, slots + 1, BLK, BLK), jnp.bfloat16),
            VM((panels, rows // panels * BLK, cols * BLK), jnp.bfloat16),
            pltpu.SemaphoreType.DMA((mats,)),
            pltpu.SemaphoreType.DMA((panels,)),
        ],
        compiler_params=params(),
        cost_estimate=cost(0, mats * (slots + rows * cols) * BLK * BLK * 2),
    )(*tables, *blocks, *earlier)


def stream(weights, stores, sem, tile, transposed, by_tile, ahead):
    length = weights[0].shape[0] if transposed else weights[0].shape[1]
    order = [(i, w) for i in range(length // tile) for w in range(len(weights))]
    if not by_tile:
        order.sort(key=lambda pair: pair[1])

    def copy(i, w):
        at = (pl.ds(i * tile, tile),) if transposed else (slice(None), pl.ds(i * tile, tile))
        return pltpu.make_async_copy(weights[w].at[at], stores[w].at[at], sem.at[w, i])

    for pair in order[:ahead]:
        copy(*pair).start()
    for n, (i, w) in enumerate(order):
        copy(i, w).wait()
        if n + ahead < len(order):
            copy(*order[n + ahead]).start()
        place = pl.ds(i * tile, tile)
        yield i, w, (stores[w].at[place] if transposed else stores[w].at[:, place])


def product(panel, held, transposed):
    dims = (((1,), (1 if transposed else 0,)), ((), ()))
    return lax.dot_general(panel, held[...], dims, preferred_element_type=jnp.float32)


def project_kernel(transposed, parts, mats, tile, core_ref, *refs):
    panels, weights = refs[:parts], refs[parts : parts + mats]
    outs = refs[-1 - mats - 2 * parts : -1 - mats]
    stores, sem = refs[-1 - mats : -1], refs[-1]
    is_first = core_ref[0] == 0
    half = panels[0].shape[0] // 2
    width = outs[0].shape[1] // mats
    panel = jnp.concatenate([ref[...] for ref in panels], axis=0)
    for i, w, held in stream(weights, stores, sem, tile, transposed, False, AHEAD):
        full = product(panel, held, transposed)
        span = slice(w * width + i * tile, w * width + (i + 1) * tile)
        for p in range(parts):
            first = full[2 * p * half : (2 * p + 1) * half]
            second = full[(2 * p + 1) * half : (2 * p + 2) * half]
            outs[2 * p][:, span] = jnp.where(is_first, first, second)
            outs[2 * p + 1][:, span] = jnp.where(is_first, second, first).astype(jnp.bfloat16)


def project(core, panels, weights, transposed, *earlier):
    parts, mats = len(panels), len(weights)
    tokens, depth = panels[0].shape
    width = weights[0].shape[0] if transposed else weights[0].shape[1]
    tile = tile_of(width, 512)
    shapes = (
        jax.ShapeDtypeStruct((tokens // 2, mats * width), jnp.float32),
        jax.ShapeDtypeStruct((tokens // 2, mats * width), jnp.bfloat16),
    )
    return pl.pallas_call(
        functools.partial(project_kernel, transposed, parts, mats, tile),
        out_shape=shapes * parts,
        in_specs=[whole(SM)]
        + [whole(VM)] * parts
        + [whole(pl.ANY)] * (mats + len(earlier)),
        out_specs=(whole(VM),) * (2 * parts),
        scratch_shapes=[VM(w.shape, jnp.bfloat16) for w in weights]
        + [pltpu.SemaphoreType.DMA((mats, width // tile))],
        compiler_params=params(),
        cost_estimate=cost(
            2 * parts * tokens * depth * width * mats, 2 * depth * width * mats
        ),
    )(core, *panels, *weights, *earlier)


def project_blocks_kernel(transposed, rows, cols, high, ring, core_ref, table, panel_ref, blocks, *refs):
    mine_ref, other_ref, dense = refs[-7:-4]
    store, stage, in_sem, out_sem = refs[-4:]
    slots = blocks.shape[0]
    load = pltpu.make_async_copy(blocks, store.at[pl.ds(0, slots)], in_sem)
    load.start()
    store[slots] = jnp.zeros((BLK, BLK), jnp.bfloat16)
    is_first = core_ref[0] == 0
    half = panel_ref.shape[0] // 2
    load.wait()
    writes = []
    for i in range((rows if transposed else cols) // high):
        held = stage.at[i % ring]
        if i >= ring:
            writes[i - ring].wait()
        for far in range(cols if transposed else rows):
            for near in range(high):
                r, c = (i * high + near, far) if transposed else (far, i * high + near)
                r_at, c_at = (near, far) if transposed else (far, near)
                held[r_at * BLK : (r_at + 1) * BLK, c_at * BLK : (c_at + 1) * BLK] = store[
                    table[r * cols + c]
                ]
        at = pl.ds(i * high * BLK, high * BLK)
        write = pltpu.make_async_copy(
            held, dense.at[at] if transposed else dense.at[:, at], out_sem.at[i % ring]
        )
        write.start()
        writes.append(write)
        full = product(panel_ref[...], held, transposed)
        first, second = full[:half], full[half:]
        mine_ref[:, at] = jnp.where(is_first, first, second)
        other_ref[:, at] = jnp.where(is_first, second, first).astype(jnp.bfloat16)
    for write in writes[-ring:]:
        write.wait()


def project_blocks(core, panel, table, blocks, rows, cols, transposed, *earlier):
    tokens, _ = panel.shape
    slots = blocks.shape[0]
    cut, across = (rows, cols) if transposed else (cols, rows)
    high = tile_of(cut * BLK, 512) // BLK
    ring = min(3, cut // high)
    tile_shape = (high * BLK, across * BLK) if transposed else (across * BLK, high * BLK)
    shape = (tokens // 2, cut * BLK)
    return pl.pallas_call(
        functools.partial(project_blocks_kernel, transposed, rows, cols, high, ring),
        out_shape=(
            jax.ShapeDtypeStruct(shape, jnp.float32),
            jax.ShapeDtypeStruct(shape, jnp.bfloat16),
            jax.ShapeDtypeStruct((rows * BLK, cols * BLK), jnp.bfloat16),
        ),
        in_specs=[whole(SM)] * 2 + [whole(VM)] + [whole(pl.ANY)] * (1 + len(earlier)),
        out_specs=(whole(VM), whole(VM), whole(pl.ANY)),
        scratch_shapes=[
            VM((slots + 1, BLK, BLK), jnp.bfloat16),
            VM((ring, *tile_shape), jnp.bfloat16),
            pltpu.SemaphoreType.DMA,
            pltpu.SemaphoreType.DMA((ring,)),
        ],
        compiler_params=params(),
        cost_estimate=cost(2 * tokens * rows * cols * BLK * BLK, rows * cols * BLK * BLK * 4),
    )(core, table, panel, blocks, *earlier)


def back_kernel(transposed, n_pieces, mats, chunks, tile, core_ref, *refs):
    pieces, weights = refs[:n_pieces], refs[n_pieces : n_pieces + mats]
    outs = refs[-1 - mats - chunks : -1 - mats]
    stores, sem = refs[-1 - mats : -1], refs[-1]
    is_first = core_ref[0] == 0
    half = pieces[0].shape[1]
    rows = n_pieces * half // chunks
    panels = [jnp.concatenate([ref[w] for ref in pieces], axis=0) for w in range(mats)]
    total = None
    for i, w, held in stream(weights, stores, sem, tile, transposed, True, AHEAD):
        part = product(panels[w], held, transposed)
        total = part if w == 0 else total + part
        if w < mats - 1:
            continue
        span = slice(i * tile, (i + 1) * tile)
        for p in range(n_pieces // 2):
            mine = total[2 * p * half : (2 * p + 1) * half]
            other = total[(2 * p + 1) * half : (2 * p + 2) * half]
            ordered = (jnp.where(is_first, mine, other), jnp.where(is_first, other, mine))
            for d in range(2 * half // rows):
                ref = outs[p * (2 * half // rows) + d]
                which, at = divmod(d * rows, half)
                ref[:, span] = ordered[which][at : at + rows].astype(ref.dtype)


def back(core, pieces, weights, chunks, transposed, *earlier):
    n_pieces, mats = len(pieces), len(weights)
    half, depth = pieces[0].shape[1:]
    width = weights[0].shape[0] if transposed else weights[0].shape[1]
    tile = tile_of(width, 512)
    rows = n_pieces * half // chunks
    shapes = tuple(
        jax.ShapeDtypeStruct((rows, width), jnp.bfloat16 if d else jnp.float32)
        for d in range(chunks)
    )
    return pl.pallas_call(
        functools.partial(back_kernel, transposed, n_pieces, mats, chunks, tile),
        out_shape=shapes,
        in_specs=[whole(SM)]
        + [whole(VM)] * n_pieces
        + [whole(pl.ANY)] * (mats + len(earlier)),
        out_specs=(whole(VM),) * chunks,
        scratch_shapes=[VM(w.shape, jnp.bfloat16) for w in weights]
        + [pltpu.SemaphoreType.DMA((mats, width // tile))],
        compiler_params=params(),
        cost_estimate=cost(
            2 * n_pieces * half * depth * width * mats, 2 * depth * width * mats
        ),
    )(core, *pieces, *weights, *earlier)


def pair_kernel(mine_ref, other_ref, *refs):
    wide = tile_of(mine_ref.shape[1], 512)
    for i in range(mine_ref.shape[1] // wide):
        span = slice(i * wide, (i + 1) * wide)
        refs[-1][:, span] = add_up([mine_ref[:, span], other_ref[:, span]]).astype(jnp.bfloat16)


def pair_sum(mine, other, *earlier):
    return pl.pallas_call(
        pair_kernel,
        out_shape=jax.ShapeDtypeStruct(mine.shape, jnp.bfloat16),
        in_specs=[whole(VM)] * 2 + [whole(pl.ANY)] * len(earlier),
        out_specs=whole(VM),
        compiler_params=params(),
        cost_estimate=cost(0, mine.size * 8),
    )(mine, other, *earlier)


def hold_kernel(*refs):
    del refs


def hold(x, *earlier):
    return pl.pallas_call(
        hold_kernel,
        out_shape=jax.ShapeDtypeStruct(x.shape, x.dtype),
        in_specs=[whole(pl.ANY)] * (1 + len(earlier)),
        out_specs=whole(pl.ANY),
        input_output_aliases={0: 0},
        compiler_params=params(),
        cost_estimate=pl.CostEstimate(flops=0, bytes_accessed=MARK, transcendentals=0),
    )(x, *earlier)


def sum_kernel(n_sum, *refs):
    refs[-1][...] = add_up([ref[...] for ref in refs[:n_sum]]).astype(refs[-1].dtype)


def sum_chunks(kept, *earlier):
    return pl.pallas_call(
        functools.partial(sum_kernel, len(kept)),
        out_shape=jax.ShapeDtypeStruct(kept[0].shape, jnp.bfloat16),
        in_specs=[whole(VM)] * len(kept) + [whole(pl.ANY)] * len(earlier),
        out_specs=whole(VM),
        compiler_params=params(),
        cost_estimate=cost(0, kept[0].size * 10),
    )(*kept, *earlier)


def mark_kernel(*refs):
    refs[-1][...] = jnp.zeros_like(refs[-1])


def mark(*earlier):
    return pl.pallas_call(
        mark_kernel,
        out_shape=jax.ShapeDtypeStruct((8, BLK), jnp.float32),
        in_specs=[whole(pl.ANY)] * len(earlier),
        out_specs=whole(VM),
        compiler_params=params(),
        cost_estimate=pl.CostEstimate(flops=0, bytes_accessed=MARK, transcendentals=0),
    )(*earlier)


def act_kernel(n_sum, *refs):
    gates, ups = refs[:n_sum], refs[n_sum : 2 * n_sum]
    hidden_ref, by_gate_ref, by_up_ref = refs[-3:]
    wide = tile_of(gates[0].shape[1], 512)
    for i in range(gates[0].shape[1] // wide):
        span = slice(i * wide, (i + 1) * wide)
        gate = add_up([ref[:, span] for ref in gates])
        up = add_up([ref[:, span] for ref in ups])
        sigma = jax.nn.sigmoid(gate)
        active = gate * sigma
        hidden_ref[0, :, span] = (active * up).astype(jnp.bfloat16)
        by_gate_ref[:, span] = up * sigma * (1.0 + gate * (1.0 - sigma))
        by_up_ref[:, span] = active


def act(gates, ups, *earlier):
    rows, width = gates[0].shape
    wide = jax.ShapeDtypeStruct((rows, width), jnp.float32)
    return pl.pallas_call(
        functools.partial(act_kernel, len(gates)),
        out_shape=(jax.ShapeDtypeStruct((1, rows, width), jnp.bfloat16), wide, wide),
        in_specs=[whole(VM)] * (2 * len(gates)) + [whole(pl.ANY)] * len(earlier),
        out_specs=(whole(VM),) * 3,
        compiler_params=params(),
        cost_estimate=cost(0, rows * width * 30),
    )(*gates, *ups, *earlier)


def grads_kernel(n_sum, *refs):
    sums, (by_gate_ref, by_up_ref) = refs[:n_sum], refs[n_sum : n_sum + 2]
    both_ref = refs[-1]
    wide = tile_of(sums[0].shape[1], 512)
    for i in range(sums[0].shape[1] // wide):
        span = slice(i * wide, (i + 1) * wide)
        grad_hidden = add_up([ref[:, span] for ref in sums])
        both_ref[0, :, span] = (grad_hidden * by_gate_ref[:, span]).astype(jnp.bfloat16)
        both_ref[1, :, span] = (grad_hidden * by_up_ref[:, span]).astype(jnp.bfloat16)


def act_grads(sums, by_gate, by_up, *earlier):
    return pl.pallas_call(
        functools.partial(grads_kernel, len(sums)),
        out_shape=jax.ShapeDtypeStruct((2, *by_gate.shape), jnp.bfloat16),
        in_specs=[whole(VM)] * (len(sums) + 2) + [whole(pl.ANY)] * len(earlier),
        out_specs=whole(VM),
        compiler_params=params(),
        cost_estimate=cost(0, by_gate.size * 20),
    )(*sums, by_gate, by_up, *earlier)


def block_grad_kernel(parts, mats, n_left, n_right, left_whole, scale, cols, wide, *refs):
    core_ref, tables, counts = refs[0], refs[1 : 1 + mats], refs[1 + mats : 1 + 2 * mats]
    rest = refs[1 + 2 * mats :]
    lefts, rights = rest[:n_left], rest[n_left : n_left + n_right]
    outs, stores = rest[-2 - 2 * mats : -2 - mats], rest[-2 - mats : -2]
    turned, sem = rest[-2:]
    core = core_ref[0]
    slots = outs[0].shape[0]
    length, width = turned.shape[0], rights[0].shape[-1]
    tall = tile_of(length, 512)

    for a in range(length // tall):
        span = slice(a * tall, (a + 1) * tall)
        if left_whole:
            pieces = [q for ref in lefts for q in natural_to_own(core, parts, ref, span)]
        else:
            pieces = [ref[0, :, span] for ref in lefts]
        turned[span, :] = jnp.concatenate(pieces, axis=0).T

    copies = []
    for m in range(mats):

        def clear(slot, carry, m=m):
            stores[m][slot] = jnp.zeros((BLK, BLK), jnp.bfloat16)
            return carry

        def column(at, carry, m=m):
            span = pl.ds(pl.multiple_of(at * wide, wide), wide)
            if left_whole:
                panel = [ref[m, :, span] for ref in rights]
            else:
                panel = [q for ref in rights for q in natural_to_own(core, parts, ref, span)]
            panel = jnp.concatenate(panel, axis=0)
            for a in range(length // tall):
                full = jnp.dot(
                    turned[a * tall : (a + 1) * tall, :], panel, preferred_element_type=jnp.float32
                )
                full = (full * scale).astype(jnp.bfloat16)
                for di in range(tall // BLK):
                    for dj in range(wide // BLK):
                        row = a * (tall // BLK) + di
                        slot = tables[m][row * cols + at * (wide // BLK) + dj]
                        stores[m][slot] = full[
                            di * BLK : (di + 1) * BLK, dj * BLK : (dj + 1) * BLK
                        ]
            return carry

        lax.fori_loop(counts[m][0], slots, clear, 0)
        lax.fori_loop(0, width // wide, column, 0)
        copies.append(
            pltpu.make_async_copy(stores[m].at[pl.ds(0, slots)], outs[m], sem.at[m])
        )
        copies[m].start()
    for copy in copies:
        copy.wait()


def block_grads(core, tables, counts, lefts, rights, left_whole, parts, slots, scale, *earlier):
    mats = len(tables)
    tokens = sum(a.shape[0] for a in (lefts if left_whole else rights))
    length, width = lefts[0].shape[-1], rights[0].shape[-1]
    wide = tile_of(width, 512)
    return pl.pallas_call(
        functools.partial(
            block_grad_kernel,
            parts,
            mats,
            len(lefts),
            len(rights),
            left_whole,
            scale,
            width // BLK,
            wide,
        ),
        out_shape=(jax.ShapeDtypeStruct((slots, BLK, BLK), jnp.bfloat16),) * mats,
        in_specs=[whole(SM)] * (1 + 2 * mats)
        + [whole(VM)] * (len(lefts) + len(rights))
        + [whole(pl.ANY)] * len(earlier),
        out_specs=(whole(pl.ANY),) * mats,
        scratch_shapes=[VM((slots + 1, BLK, BLK), jnp.bfloat16)] * mats
        + [VM((length, tokens), jnp.bfloat16), pltpu.SemaphoreType.DMA((mats,))],
        compiler_params=params(),
        cost_estimate=cost(2 * tokens * length * width * mats, slots * BLK * BLK * 2 * mats),
    )(core, *tables, *counts, *lefts, *rights, *earlier)


def shift(x, axis, by):
    n = lax.axis_size(axis)
    return lax.ppermute(x, axis, [(i, (i + by) % n) for i in range(n)])


def swap_cores(x):
    n = lax.axis_size("row")
    return lax.ppermute(x, "row", [(i, i ^ 1) for i in range(n)])


def add_up(parts):
    total = parts[0].astype(jnp.float32)
    for part in parts[1:]:
        total = total + part.astype(jnp.float32)
    return total


def z_order(n):
    return sorted(range(1, n), key=lambda d: (min(d, n - d), d))


def other_chips(sent):
    n = lax.axis_size("row")
    return [shift(sent, "row", 2 * s) for s in range(1, n // 2)]


def other_groups(x):
    return [shift(x, "dp", s) for s in range(1, lax.axis_size("dp"))]


def on_device(
    tokens, cotangent, gate_blocks, gate_index, up_blocks, up_index, down_blocks, down_index
):
    n_col = lax.axis_size("col")
    parts = 1
    chunks = n_col // parts
    core = lax.rem(lax.axis_index("row"), 2).astype(jnp.int32).reshape(1)
    feats = tokens.shape[1] // BLK
    units = FF // BLK // n_col
    width = units * BLK
    slots = gate_blocks.shape[2]
    group_rows = tokens.shape[0] * n_col
    scale = 1.0 / math.sqrt(group_rows * lax.axis_size("dp"))

    def gather(x):
        got = {0: x}
        for d in z_order(n_col):
            got[d] = shift(x, "col", d)
        return [
            jnp.concatenate([got[d] for d in range(p * chunks, (p + 1) * chunks)], axis=0)
            for p in range(parts)
        ]

    def scatter(cut, *earlier):
        kept = [cut[0]] + [shift(cut[d], "col", -d) for d in z_order(n_col)]
        return sum_chunks(kept, *earlier)

    def far_pieces(pairs):
        pieces = []
        for s in range(lax.axis_size("dp") - 1):
            for far in pairs:
                pieces += [far[s], swap_cores(far[s])]
        return pieces

    gate_table, gate_count = slot_table(gate_index, feats, units)
    up_table, up_count = slot_table(up_index, feats, units)
    down_table, down_count = slot_table(down_index, units, feats)

    x_parts = gather(tokens)
    x_whole = jnp.concatenate(x_parts, axis=0)
    (w_gate,) = densify((gate_table,), (gate_blocks[0, 0],), feats, units)
    gate_mine, gate_other = project(core, x_parts, [w_gate], False)
    gate_swapped = swap_cores(gate_other)
    gate_sent = pair_sum(gate_mine, gate_swapped)

    gate_got = other_chips(gate_sent)
    c_parts = gather(after(cotangent, x_whole))
    c_whole = jnp.concatenate(c_parts, axis=0)
    x_groups = [x_whole] + other_groups(x_whole)
    up_mine, up_other, w_up = project_blocks(
        core, x_whole, up_table, up_blocks[0, 0], feats, units, False, gate_sent
    )
    token = mark(up_other, *gate_got, c_whole, *x_groups[1:])
    up_swapped = swap_cores(up_other)
    up_sent = pair_sum(up_mine, up_swapped, token)

    up_got = other_chips(up_sent)
    c_groups = [c_whole] + other_groups(c_whole)
    back_mine, back_other, w_down = project_blocks(
        core, c_whole, down_table, down_blocks[0, 0], units, feats, True, up_sent
    )
    token = mark(back_other, *up_got, *c_groups[1:])
    hidden, by_gate, by_up = act(
        [gate_mine, gate_swapped] + gate_got, [up_mine, up_swapped] + up_got, token
    )
    back_swapped = swap_cores(back_other)
    back_sent = pair_sum(back_mine, back_swapped, hidden)

    back_got = other_chips(back_sent)
    hidden_far = other_groups(hidden)
    hidden_pieces = [hidden, swap_cores(hidden)]
    out_cut = back(core, hidden_pieces, [w_down], n_col, False, back_sent)
    hidden_far = [hold(far, out_cut[0]) for far in hidden_far]
    hidden_pieces += far_pieces([hidden_far])
    token = mark(out_cut[0], *back_got, *hidden_pieces[2:])
    grads = act_grads([back_mine, back_swapped] + back_got, by_gate, by_up, token)

    grads_far = other_groups(grads)
    grad_pieces = [grads, swap_cores(grads)]
    (down_grad,) = block_grads(
        core,
        (down_table,),
        (down_count,),
        hidden_pieces,
        c_groups,
        False,
        parts,
        slots,
        scale,
        grad_pieces[1],
    )
    in_cut = back(core, grad_pieces, [w_gate, w_up], n_col, True, down_grad)
    output = scatter(out_cut, in_cut[0])
    grads_far = [hold(far, output) for far in grads_far]
    gate_grad, up_grad = block_grads(
        core,
        (gate_table, up_table),
        (gate_count, up_count),
        x_groups,
        grad_pieces + far_pieces([grads_far]),
        True,
        parts,
        slots,
        scale,
    )
    input_grad = scatter(in_cut, gate_grad)
    shape = gate_blocks.shape
    return (
        output,
        input_grad,
        gate_grad.reshape(shape),
        up_grad.reshape(shape),
        down_grad.reshape(shape),
    )


def solution(mesh):
    return jax.shard_map(
        on_device,
        mesh=mesh,
        in_specs=(
            P(("dp", "col"), "row"),
            P(("dp", "col"), "row"),
            P("row", "col", None, None, None),
            P("row", "col", None, None),
            P("row", "col", None, None, None),
            P("row", "col", None, None),
            P("row", "col", None, None, None),
            P("row", "col", None, None),
        ),
        out_specs=(
            P(("dp", "col"), "row"),
            P(("dp", "col"), "row"),
            P("row", "col", None, None, None),
            P("row", "col", None, None, None),
            P("row", "col", None, None, None),
        ),
        check_vma=False,
    )
```

```python
import functools
import math

import jax
import jax.numpy as jnp
from jax import lax
from jax.experimental import pallas as pl
from jax.experimental.pallas import tpu as pltpu
from jax.sharding import PartitionSpec as P

BLK = 128
AHEAD = 3
PROJECT_TILE = 512
BACK_TILE = 512
GRAD_WIDE = 512
POINT_WIDE = 1792
COST = 0.000001
MARK = 200000
FF = 14336
VMEM_LIMIT = 56 * 1024 * 1024
VM = pltpu.VMEM
SM = pltpu.SMEM


def params():
    return pltpu.CompilerParams(vmem_limit_bytes=VMEM_LIMIT)


def cost(flops, nbytes):
    return pl.CostEstimate(
        flops=int(flops * COST), bytes_accessed=int(nbytes * COST), transcendentals=0
    )


def tile_of(size, largest):
    return max(t for t in range(BLK, largest + 1, BLK) if size % t == 0)


def rows_at(start, rows):
    return pl.ds(pl.multiple_of(start, rows), rows)


def whole(memory_space):
    return pl.BlockSpec(memory_space=memory_space)


def after(x, *earlier):
    return lax.optimization_barrier((x, *earlier))[0]


def slot_table(index_list, first_count, second_count):
    listing = index_list[0, 0]
    slots = listing.shape[0]
    flat = jnp.where(listing[:, 0] >= 0, listing[:, 0] * second_count + listing[:, 1], -1)
    positions = jnp.arange(first_count * second_count, dtype=jnp.int32)
    hits = flat[None, :] == positions[:, None]
    back_from = slots - jnp.arange(slots, dtype=jnp.int32)
    table = slots - jnp.sum(jnp.where(hits, back_from[None, :], 0), axis=1)
    count = jnp.sum((flat >= 0).astype(jnp.int32))
    return table, count.reshape(1)


def densify_kernel(mats, rows, cols, panels, *refs):
    tables, blocks = refs[:mats], refs[mats : 2 * mats]
    outs = refs[-4 - mats : -4]
    store, stage, in_sem, out_sem = refs[-4:]
    slots = blocks[0].shape[0]
    loads = [
        pltpu.make_async_copy(blocks[m], store.at[m, pl.ds(0, slots)], in_sem.at[m])
        for m in range(mats)
    ]
    for load in loads:
        load.start()
    high = rows // panels
    writes = []
    for m in range(mats):
        store[m, slots] = jnp.zeros((BLK, BLK), jnp.bfloat16)
        loads[m].wait()
        for g in range(panels):
            if m:
                writes[(m - 1) * panels + g].wait()

            def fill(r, carry, m=m, g=g):
                for j in range(cols):
                    slot = tables[m][(g * high + r) * cols + j]
                    stage[g, rows_at(r * BLK, BLK), j * BLK : (j + 1) * BLK] = store[m, slot]
                return carry

            lax.fori_loop(0, high, fill, 0)
            write = pltpu.make_async_copy(
                stage.at[g], outs[m].at[pl.ds(g * high * BLK, high * BLK)], out_sem.at[g]
            )
            write.start()
            writes.append(write)
    for write in writes[-panels:]:
        write.wait()


def densify(tables, blocks, rows, cols, *earlier):
    mats = len(blocks)
    slots = blocks[0].shape[0]
    panels = 4 if rows % 4 == 0 else 1
    shape = jax.ShapeDtypeStruct((rows * BLK, cols * BLK), jnp.bfloat16)
    return pl.pallas_call(
        functools.partial(densify_kernel, mats, rows, cols, panels),
        out_shape=(shape,) * mats,
        in_specs=[whole(SM)] * mats + [whole(pl.ANY)] * (mats + len(earlier)),
        out_specs=(whole(pl.ANY),) * mats,
        scratch_shapes=[
            VM((mats, slots + 1, BLK, BLK), jnp.bfloat16),
            VM((panels, rows // panels * BLK, cols * BLK), jnp.bfloat16),
            pltpu.SemaphoreType.DMA((mats,)),
            pltpu.SemaphoreType.DMA((panels,)),
        ],
        compiler_params=params(),
        cost_estimate=cost(0, mats * (slots + rows * cols) * BLK * BLK * 2),
    )(*tables, *blocks, *earlier)


def stream(copies, first):
    for copy in first:
        copy.start()
    copies[0].start()
    for copy in first:
        copy.wait()
    for n, copy in enumerate(copies):
        if n == 0:
            for ahead in copies[1:AHEAD]:
                ahead.start()
        copy.wait()
        if n + AHEAD < len(copies):
            copies[n + AHEAD].start()
        yield n


def product(panel, held, transposed):
    dims = (((1,), (1 if transposed else 0,)), ((), ()))
    return lax.dot_general(panel, held[...], dims, preferred_element_type=jnp.float32)


def project_kernel(transposed, tile, core_ref, panel, weight, *refs):
    mine_ref, other_ref = refs[-5:-3]
    held_panel, store, sem = refs[-3:]
    load = pltpu.make_async_copy(panel, held_panel, sem.at[0])
    is_first = core_ref[0] == 0
    half = panel.shape[0] // 2
    spans = [pl.ds(i * tile, tile) for i in range(mine_ref.shape[1] // tile)]
    places = [(at,) if transposed else (slice(None), at) for at in spans]
    copies = [
        pltpu.make_async_copy(weight.at[at], store.at[at], sem.at[1 + i])
        for i, at in enumerate(places)
    ]
    for i in stream(copies, [load]):
        full = product(held_panel[...], store.at[places[i]], transposed)
        first, second = full[:half], full[half:]
        mine_ref[:, spans[i]] = jnp.where(is_first, first, second)
        other_ref[:, spans[i]] = jnp.where(is_first, second, first).astype(jnp.bfloat16)


def project(core, panel, weight, transposed, *earlier):
    tokens, depth = panel.shape
    width = weight.shape[0] if transposed else weight.shape[1]
    tile = tile_of(width, PROJECT_TILE)
    shape = (tokens // 2, width)
    return pl.pallas_call(
        functools.partial(project_kernel, transposed, tile),
        out_shape=(
            jax.ShapeDtypeStruct(shape, jnp.float32),
            jax.ShapeDtypeStruct(shape, jnp.bfloat16),
        ),
        in_specs=[whole(SM)] + [whole(pl.ANY)] * (2 + len(earlier)),
        out_specs=(whole(VM),) * 2,
        scratch_shapes=[
            VM(panel.shape, jnp.bfloat16),
            VM(weight.shape, jnp.bfloat16),
            pltpu.SemaphoreType.DMA((1 + width // tile,)),
        ],
        compiler_params=params(),
        cost_estimate=cost(2 * tokens * depth * width, 2 * depth * width),
    )(core, panel, weight, *earlier)


def project_blocks_kernel(transposed, rows, cols, high, ring, core_ref, table, panel, blocks, *refs):
    mine_ref, other_ref, dense = refs[-8:-5]
    store, panel_ref, stage, in_sem, out_sem = refs[-5:]
    slots = blocks.shape[0]
    load = pltpu.make_async_copy(blocks, store.at[pl.ds(0, slots)], in_sem.at[0])
    load.start()
    load_panel = pltpu.make_async_copy(panel, panel_ref, in_sem.at[1])
    load_panel.start()
    store[slots] = jnp.zeros((BLK, BLK), jnp.bfloat16)
    is_first = core_ref[0] == 0
    half = panel_ref.shape[0] // 2
    load.wait()
    load_panel.wait()
    writes = []
    for i in range((rows if transposed else cols) // high):
        held = stage.at[i % ring]
        if i >= ring:
            writes[i - ring].wait()
        for far in range(cols if transposed else rows):
            for near in range(high):
                r, c = (i * high + near, far) if transposed else (far, i * high + near)
                r_at, c_at = (near, far) if transposed else (far, near)
                held[r_at * BLK : (r_at + 1) * BLK, c_at * BLK : (c_at + 1) * BLK] = store[
                    table[r * cols + c]
                ]
        at = pl.ds(i * high * BLK, high * BLK)
        write = pltpu.make_async_copy(
            held, dense.at[at] if transposed else dense.at[:, at], out_sem.at[i % ring]
        )
        write.start()
        writes.append(write)
        full = product(panel_ref[...], held, transposed)
        first, second = full[:half], full[half:]
        mine_ref[:, at] = jnp.where(is_first, first, second)
        other_ref[:, at] = jnp.where(is_first, second, first).astype(jnp.bfloat16)
    for write in writes[-ring:]:
        write.wait()


def project_blocks(core, panel, table, blocks, rows, cols, transposed, *earlier):
    tokens, _ = panel.shape
    slots = blocks.shape[0]
    cut, across = (rows, cols) if transposed else (cols, rows)
    high = tile_of(cut * BLK, 512) // BLK
    ring = min(3, cut // high)
    tile_shape = (high * BLK, across * BLK) if transposed else (across * BLK, high * BLK)
    shape = (tokens // 2, cut * BLK)
    return pl.pallas_call(
        functools.partial(project_blocks_kernel, transposed, rows, cols, high, ring),
        out_shape=(
            jax.ShapeDtypeStruct(shape, jnp.float32),
            jax.ShapeDtypeStruct(shape, jnp.bfloat16),
            jax.ShapeDtypeStruct((rows * BLK, cols * BLK), jnp.bfloat16),
        ),
        in_specs=[whole(SM)] * 2 + [whole(pl.ANY)] * (2 + len(earlier)),
        out_specs=(whole(VM), whole(VM), whole(pl.ANY)),
        scratch_shapes=[
            VM((slots + 1, BLK, BLK), jnp.bfloat16),
            VM(panel.shape, jnp.bfloat16),
            VM((ring, *tile_shape), jnp.bfloat16),
            pltpu.SemaphoreType.DMA((2,)),
            pltpu.SemaphoreType.DMA((ring,)),
        ],
        compiler_params=params(),
        cost_estimate=cost(2 * tokens * rows * cols * BLK * BLK, rows * cols * BLK * BLK * 4),
    )(core, table, panel, blocks, *earlier)


def back_kernel(transposed, n_pieces, mats, chunks, tile, core_ref, *refs):
    pieces, weights = refs[:n_pieces], refs[n_pieces : n_pieces + mats]
    outs = refs[-4 - chunks : -4]
    store, panel, sem, piece_sem = refs[-4:]
    half, depth = pieces[0].shape[1:]
    loads = [
        pltpu.make_async_copy(
            piece.at[w],
            panel.at[pl.ds(k * half, half), pl.ds(w * depth, depth)],
            piece_sem.at[w * n_pieces + k],
        )
        for w in range(mats)
        for k, piece in enumerate(pieces)
    ]
    is_first = core_ref[0] == 0
    rows = n_pieces * half // chunks
    copies = []
    for i in range(outs[0].shape[1] // tile):
        at = pl.ds(i * tile, tile)
        for w, weight in enumerate(weights):
            deep = pl.ds(w * depth, depth)
            source = weight.at[at] if transposed else weight.at[:, at]
            target = store.at[at, deep] if transposed else store.at[deep, at]
            copies.append(pltpu.make_async_copy(source, target, sem.at[w, i]))
    for n in stream(copies, loads):
        if n % mats < mats - 1:
            continue
        at = pl.ds(n // mats * tile, tile)
        total = product(panel[...], store.at[at] if transposed else store.at[:, at], transposed)
        mine, other = total[:half], total[half:]
        ordered = (jnp.where(is_first, mine, other), jnp.where(is_first, other, mine))
        for d in range(chunks):
            which, start = divmod(d * rows, half)
            outs[d][:, at] = ordered[which][start : start + rows].astype(outs[d].dtype)


def back(core, pieces, weights, chunks, transposed, *earlier):
    n_pieces, mats = len(pieces), len(weights)
    half, depth = pieces[0].shape[1:]
    width = weights[0].shape[0] if transposed else weights[0].shape[1]
    tile = tile_of(width, BACK_TILE)
    rows = n_pieces * half // chunks
    shapes = tuple(
        jax.ShapeDtypeStruct((rows, width), jnp.bfloat16 if d else jnp.float32)
        for d in range(chunks)
    )
    return pl.pallas_call(
        functools.partial(back_kernel, transposed, n_pieces, mats, chunks, tile),
        out_shape=shapes,
        in_specs=[whole(SM)] + [whole(pl.ANY)] * (n_pieces + mats + len(earlier)),
        out_specs=(whole(VM),) * chunks,
        scratch_shapes=[
            VM((width, mats * depth) if transposed else (mats * depth, width), jnp.bfloat16),
            VM((n_pieces * half, mats * depth), jnp.bfloat16),
            pltpu.SemaphoreType.DMA((mats, width // tile)),
            pltpu.SemaphoreType.DMA((mats * n_pieces,)),
        ],
        compiler_params=params(),
        cost_estimate=cost(
            2 * n_pieces * half * depth * width * mats, 2 * depth * width * mats
        ),
    )(core, *pieces, *weights, *earlier)


def pair_kernel(mine_ref, other_ref, *refs):
    wide = tile_of(mine_ref.shape[1], 512)
    for i in range(mine_ref.shape[1] // wide):
        span = slice(i * wide, (i + 1) * wide)
        refs[-1][:, span] = add_up([mine_ref[:, span], other_ref[:, span]]).astype(jnp.bfloat16)


def pair_sum(mine, other, *earlier):
    return pl.pallas_call(
        pair_kernel,
        out_shape=jax.ShapeDtypeStruct(mine.shape, jnp.bfloat16),
        in_specs=[whole(VM)] * 2 + [whole(pl.ANY)] * len(earlier),
        out_specs=whole(VM),
        compiler_params=params(),
        cost_estimate=cost(0, mine.size * 8),
    )(mine, other, *earlier)


def hold_kernel(*refs):
    del refs


def hold(x, *earlier):
    return pl.pallas_call(
        hold_kernel,
        out_shape=jax.ShapeDtypeStruct(x.shape, x.dtype),
        in_specs=[whole(pl.ANY)] * (1 + len(earlier)),
        out_specs=whole(pl.ANY),
        input_output_aliases={0: 0},
        compiler_params=params(),
        cost_estimate=pl.CostEstimate(flops=0, bytes_accessed=MARK, transcendentals=0),
    )(x, *earlier)


def sum_kernel(counts, *refs):
    at = 0
    for out, count in zip(refs[len(refs) - len(counts) :], counts):
        out[...] = add_up([ref[...] for ref in refs[at : at + count]]).astype(out.dtype)
        at += count


def sum_chunks(lists, *earlier):
    counts = [len(parts) for parts in lists]
    parts = [part for parts in lists for part in parts]
    return pl.pallas_call(
        functools.partial(sum_kernel, counts),
        out_shape=tuple(jax.ShapeDtypeStruct(p[0].shape, jnp.bfloat16) for p in lists),
        in_specs=[whole(VM)] * len(parts) + [whole(pl.ANY)] * len(earlier),
        out_specs=(whole(VM),) * len(lists),
        compiler_params=params(),
        cost_estimate=cost(0, parts[0].size * 10),
    )(*parts, *earlier)


def mark_kernel(*refs):
    refs[-1][...] = jnp.zeros_like(refs[-1])


def mark(*earlier):
    return pl.pallas_call(
        mark_kernel,
        out_shape=jax.ShapeDtypeStruct((8, BLK), jnp.float32),
        in_specs=[whole(pl.ANY)] * len(earlier),
        out_specs=whole(VM),
        compiler_params=params(),
        cost_estimate=pl.CostEstimate(flops=0, bytes_accessed=MARK, transcendentals=0),
    )(*earlier)


def across(rows, width):
    return pl.BlockSpec((rows, tile_of(width, POINT_WIDE)), lambda i: (0, i))


def act_kernel(n_sum, *refs):
    gates, ups = refs[:n_sum], refs[n_sum : 2 * n_sum]
    hidden_ref, by_gate_ref, by_up_ref = refs[-3:]
    span = slice(None)
    gate = add_up([ref[:, span] for ref in gates])
    up = add_up([ref[:, span] for ref in ups])
    sigma = jax.nn.sigmoid(gate)
    active = gate * sigma
    hidden_ref[0, :, span] = (active * up).astype(jnp.bfloat16)
    by_gate_ref[:, span] = up * sigma * (1.0 + gate * (1.0 - sigma))
    by_up_ref[:, span] = active


def act(gates, ups, *earlier):
    rows, width = gates[0].shape
    wide = jax.ShapeDtypeStruct((rows, width), jnp.float32)
    return pl.pallas_call(
        functools.partial(act_kernel, len(gates)),
        out_shape=(jax.ShapeDtypeStruct((1, rows, width), jnp.bfloat16), wide, wide),
        grid=(width // tile_of(width, POINT_WIDE),),
        in_specs=[across(rows, width)] * (2 * len(gates)) + [whole(pl.ANY)] * len(earlier),
        out_specs=(
            pl.BlockSpec((1, rows, tile_of(width, POINT_WIDE)), lambda i: (0, 0, i)),
            across(rows, width),
            across(rows, width),
        ),
        compiler_params=params(),
        cost_estimate=cost(0, rows * width * 30),
    )(*gates, *ups, *earlier)


def grads_kernel(n_sum, *refs):
    sums, (by_gate_ref, by_up_ref) = refs[:n_sum], refs[n_sum : n_sum + 2]
    both_ref = refs[-1]
    span = slice(None)
    grad_hidden = add_up([ref[:, span] for ref in sums])
    both_ref[0, :, span] = (grad_hidden * by_gate_ref[:, span]).astype(jnp.bfloat16)
    both_ref[1, :, span] = (grad_hidden * by_up_ref[:, span]).astype(jnp.bfloat16)


def act_grads(sums, by_gate, by_up, *earlier):
    return pl.pallas_call(
        functools.partial(grads_kernel, len(sums)),
        out_shape=jax.ShapeDtypeStruct((2, *by_gate.shape), jnp.bfloat16),
        grid=(by_gate.shape[1] // tile_of(by_gate.shape[1], POINT_WIDE),),
        in_specs=[across(*by_gate.shape)] * (len(sums) + 2) + [whole(pl.ANY)] * len(earlier),
        out_specs=pl.BlockSpec(
            (2, by_gate.shape[0], tile_of(by_gate.shape[1], POINT_WIDE)), lambda i: (0, 0, i)
        ),
        compiler_params=params(),
        cost_estimate=cost(0, by_gate.size * 20),
    )(*sums, by_gate, by_up, *earlier)


def own_order(core, ref):
    half = ref.shape[0] // 2
    return [ref.at[rows_at(core * half, half)], ref.at[rows_at((1 - core) * half, half)]]


def block_grad_kernel(mats, n_left, n_right, scale, cols, wide, core_ref, *refs):
    tables, counts = refs[:mats], refs[mats : 2 * mats]
    lefts = refs[2 * mats : 2 * mats + n_left]
    rights = refs[2 * mats + n_left : 2 * mats + n_left + n_right]
    outs, stores = refs[-6 - 2 * mats : -6 - mats], refs[-6 - mats : -6]
    left, right, turned, in_sem, left_sem, out_sem = refs[-6:]
    core = core_ref[0]
    slots = outs[0].shape[0]
    length, width = left.shape[1], right.shape[2]
    tall = tile_of(length, 512)

    def rows_of(refs, m):
        rows = []
        for ref in refs:
            rows += own_order(core, ref) if len(ref.shape) == 2 else [ref.at[m]]
        return rows

    def loads(sources, target, sem):
        rows = sources[0].shape[0]
        copies = [
            pltpu.make_async_copy(source, target.at[pl.ds(k * rows, rows)], sem.at[k])
            for k, source in enumerate(sources)
        ]
        return copies

    left_loads = loads(rows_of(lefts, 0), left, left_sem)
    right_loads = [loads(rows_of(rights, m), right.at[m], in_sem.at[m]) for m in range(mats)]
    for load in left_loads:
        load.start()

    def clear(slot, carry, m):
        stores[m][slot] = jnp.zeros((BLK, BLK), jnp.bfloat16)
        return carry

    for m in range(mats):
        lax.fori_loop(counts[m][0], slots, functools.partial(clear, m=m), 0)
    for load in left_loads:
        load.wait()
    for load in right_loads[0]:
        load.start()
    for a in range(length // tall):
        span = slice(a * tall, (a + 1) * tall)
        turned[span, :] = left[:, span].T

    copies = []
    for m in range(mats):
        for load in right_loads[m]:
            load.wait()
        if m + 1 < mats:
            for load in right_loads[m + 1]:
                load.start()

        def column(at, carry, m=m):
            span = pl.ds(pl.multiple_of(at * wide, wide), wide)
            for a in range(length // tall):
                full = jnp.dot(
                    turned[a * tall : (a + 1) * tall, :],
                    right[m, :, span],
                    preferred_element_type=jnp.float32,
                )
                full = (full * scale).astype(jnp.bfloat16)
                for di in range(tall // BLK):
                    for dj in range(wide // BLK):
                        row = a * (tall // BLK) + di
                        slot = tables[m][row * cols + at * (wide // BLK) + dj]
                        stores[m][slot] = full[
                            di * BLK : (di + 1) * BLK, dj * BLK : (dj + 1) * BLK
                        ]
            return carry

        lax.fori_loop(0, width // wide, column, 0)
        copies.append(
            pltpu.make_async_copy(stores[m].at[pl.ds(0, slots)], outs[m], out_sem.at[m])
        )
        copies[m].start()
    for copy in copies:
        copy.wait()


def block_grads(core, tables, counts, lefts, rights, slots, scale, *earlier):
    mats = len(tables)
    tokens = sum(a.shape[-2] for a in lefts)
    length, width = lefts[0].shape[-1], rights[0].shape[-1]
    wide = tile_of(width, GRAD_WIDE)
    n_rows = [sum(2 if a.ndim == 2 else 1 for a in side) for side in (lefts, rights)]
    return pl.pallas_call(
        functools.partial(
            block_grad_kernel,
            mats,
            len(lefts),
            len(rights),
            scale,
            width // BLK,
            wide,
        ),
        out_shape=(jax.ShapeDtypeStruct((slots, BLK, BLK), jnp.bfloat16),) * mats,
        in_specs=[whole(SM)] * (1 + 2 * mats)
        + [whole(pl.ANY)] * (len(lefts) + len(rights) + len(earlier)),
        out_specs=(whole(pl.ANY),) * mats,
        scratch_shapes=[VM((slots + 1, BLK, BLK), jnp.bfloat16)] * mats
        + [
            VM((tokens, length), jnp.bfloat16),
            VM((mats, tokens, width), jnp.bfloat16),
            VM((length, tokens), jnp.bfloat16),
            pltpu.SemaphoreType.DMA((mats, n_rows[1])),
            pltpu.SemaphoreType.DMA((n_rows[0],)),
            pltpu.SemaphoreType.DMA((mats,)),
        ],
        compiler_params=params(),
        cost_estimate=cost(2 * tokens * length * width * mats, slots * BLK * BLK * 2 * mats),
    )(core, *tables, *counts, *lefts, *rights, *earlier)


def shift(x, axis, by):
    n = lax.axis_size(axis)
    return lax.ppermute(x, axis, [(i, (i + by) % n) for i in range(n)])


def swap_cores(x):
    n = lax.axis_size("row")
    return lax.ppermute(x, "row", [(i, i ^ 1) for i in range(n)])


def add_up(parts):
    total = parts[0].astype(jnp.float32)
    for part in parts[1:]:
        total = total + part.astype(jnp.float32)
    return total


def z_order(n):
    return sorted(range(1, n), key=lambda d: (min(d, n - d), d))


def other_chips(sent):
    n = lax.axis_size("row")
    return [shift(sent, "row", 2 * s) for s in range(1, n // 2)]


def other_groups(x):
    return [shift(x, "dp", s) for s in range(1, lax.axis_size("dp"))]


def on_device(
    tokens, cotangent, gate_blocks, gate_index, up_blocks, up_index, down_blocks, down_index
):
    n_col = lax.axis_size("col")
    parts = 1
    chunks = n_col // parts
    core = lax.rem(lax.axis_index("row"), 2).astype(jnp.int32).reshape(1)
    feats = tokens.shape[1] // BLK
    units = FF // BLK // n_col
    width = units * BLK
    slots = gate_blocks.shape[2]
    group_rows = tokens.shape[0] * n_col
    scale = 1.0 / math.sqrt(group_rows * lax.axis_size("dp"))

    def gather(x):
        got = {0: x}
        for d in z_order(n_col):
            got[d] = shift(x, "col", d)
        return [
            jnp.concatenate([got[d] for d in range(p * chunks, (p + 1) * chunks)], axis=0)
            for p in range(parts)
        ]

    def scatter(cut):
        return [cut[0]] + [shift(cut[d], "col", -d) for d in z_order(n_col)]

    def far_pieces(pairs):
        pieces = []
        for s in range(lax.axis_size("dp") - 1):
            for far in pairs:
                pieces += [far[s], swap_cores(far[s])]
        return pieces

    gate_table, gate_count = slot_table(gate_index, feats, units)
    up_table, up_count = slot_table(up_index, feats, units)
    down_table, down_count = slot_table(down_index, units, feats)

    x_parts = gather(tokens)
    x_whole = jnp.concatenate(x_parts, axis=0)
    (w_gate,) = densify((gate_table,), (gate_blocks[0, 0],), feats, units)
    gate_mine, gate_other = project(core, x_whole, w_gate, False)
    gate_swapped = swap_cores(gate_other)
    gate_sent = pair_sum(gate_mine, gate_swapped)

    gate_got = other_chips(gate_sent)
    c_parts = gather(after(cotangent, x_whole))
    c_whole = jnp.concatenate(c_parts, axis=0)
    x_groups = [x_whole] + other_groups(x_whole)
    up_mine, up_other, w_up = project_blocks(
        core, x_whole, up_table, up_blocks[0, 0], feats, units, False, gate_sent
    )
    token = mark(up_other, *gate_got, c_whole, *x_groups[1:])
    up_swapped = swap_cores(up_other)
    up_sent = pair_sum(up_mine, up_swapped, token)

    up_got = other_chips(up_sent)
    c_groups = [c_whole] + other_groups(c_whole)
    back_mine, back_other, w_down = project_blocks(
        core, c_whole, down_table, down_blocks[0, 0], units, feats, True, up_sent
    )
    token = mark(back_other, *up_got, *c_groups[1:])
    back_swapped = swap_cores(back_other)
    back_sent = pair_sum(back_mine, back_swapped, token)

    back_got = other_chips(back_sent)
    hidden, by_gate, by_up = act(
        [gate_mine, gate_swapped] + gate_got, [up_mine, up_swapped] + up_got, back_sent
    )
    hidden_far = other_groups(hidden)
    hidden_pieces = [hidden, swap_cores(hidden)]
    out_cut = back(core, hidden_pieces, [w_down], n_col, False)
    token = mark(out_cut[0], *back_got)
    grads = act_grads([back_mine, back_swapped] + back_got, by_gate, by_up, token)
    hidden_pieces += far_pieces([[hold(far, grads) for far in hidden_far]])

    grads_far = other_groups(grads)
    grad_pieces = [grads, swap_cores(grads)]
    (down_grad,) = block_grads(
        core,
        (down_table,),
        (down_count,),
        hidden_pieces,
        c_groups,
        slots,
        scale,
        grad_pieces[1],
    )
    in_cut = back(core, grad_pieces, [w_gate, w_up], n_col, True, down_grad)
    out_kept = scatter(out_cut)
    grads_far = [hold(far, in_cut[0], *out_kept[1:]) for far in grads_far]
    gate_grad, up_grad = block_grads(
        core,
        (gate_table, up_table),
        (gate_count, up_count),
        x_groups,
        grad_pieces + far_pieces([grads_far]),
        slots,
        scale,
    )
    output, input_grad = sum_chunks([out_kept, scatter(in_cut)], gate_grad)
    shape = gate_blocks.shape
    return (
        output,
        input_grad,
        gate_grad.reshape(shape),
        up_grad.reshape(shape),
        down_grad.reshape(shape),
    )


def solution(mesh):
    return jax.shard_map(
        on_device,
        mesh=mesh,
        in_specs=(
            P(("dp", "col"), "row"),
            P(("dp", "col"), "row"),
            P("row", "col", None, None, None),
            P("row", "col", None, None),
            P("row", "col", None, None, None),
            P("row", "col", None, None),
            P("row", "col", None, None, None),
            P("row", "col", None, None),
        ),
        out_specs=(
            P(("dp", "col"), "row"),
            P(("dp", "col"), "row"),
            P("row", "col", None, None, None),
            P("row", "col", None, None, None),
            P("row", "col", None, None, None),
        ),
        check_vma=False,
    )
```

```python
import functools
import math

import jax
import jax.numpy as jnp
from jax import lax
from jax.experimental import pallas as pl
from jax.experimental.pallas import tpu as pltpu
from jax.sharding import PartitionSpec as P

BLK = 128
AHEAD = 3
PROJECT_TILE = 512
BACK_TILE = 512
GRAD_WIDE = 512
POINT_WIDE = 1792
COST = 0.000001
MARK = 200000
FF = 14336
VMEM_LIMIT = 56 * 1024 * 1024
VM = pltpu.VMEM
SM = pltpu.SMEM


def params():
    return pltpu.CompilerParams(vmem_limit_bytes=VMEM_LIMIT)


def cost(flops, nbytes):
    return pl.CostEstimate(
        flops=int(flops * COST), bytes_accessed=int(nbytes * COST), transcendentals=0
    )


def tile_of(size, largest):
    return max(t for t in range(BLK, largest + 1, BLK) if size % t == 0)


def rows_at(start, rows):
    return pl.ds(pl.multiple_of(start, rows), rows)


def whole(memory_space):
    return pl.BlockSpec(memory_space=memory_space)


def after(x, *earlier):
    return lax.optimization_barrier((x, *earlier))[0]


def slot_table(index_list, first_count, second_count):
    listing = index_list[0, 0]
    slots = listing.shape[0]
    flat = jnp.where(listing[:, 0] >= 0, listing[:, 0] * second_count + listing[:, 1], -1)
    positions = jnp.arange(first_count * second_count, dtype=jnp.int32)
    hits = flat[None, :] == positions[:, None]
    back_from = slots - jnp.arange(slots, dtype=jnp.int32)
    table = slots - jnp.sum(jnp.where(hits, back_from[None, :], 0), axis=1)
    count = jnp.sum((flat >= 0).astype(jnp.int32))
    return table, count.reshape(1)


def densify_kernel(mats, rows, cols, panels, *refs):
    tables, blocks = refs[:mats], refs[mats : 2 * mats]
    outs = refs[-4 - mats : -4]
    store, stage, in_sem, out_sem = refs[-4:]
    slots = blocks[0].shape[0]
    loads = [
        pltpu.make_async_copy(blocks[m], store.at[m, pl.ds(0, slots)], in_sem.at[m])
        for m in range(mats)
    ]
    for load in loads:
        load.start()
    high = rows // panels
    writes = []
    for m in range(mats):
        store[m, slots] = jnp.zeros((BLK, BLK), jnp.bfloat16)
        loads[m].wait()
        for g in range(panels):
            if m:
                writes[(m - 1) * panels + g].wait()

            def fill(r, carry, m=m, g=g):
                for j in range(cols):
                    slot = tables[m][(g * high + r) * cols + j]
                    stage[g, rows_at(r * BLK, BLK), j * BLK : (j + 1) * BLK] = store[m, slot]
                return carry

            lax.fori_loop(0, high, fill, 0)
            write = pltpu.make_async_copy(
                stage.at[g], outs[m].at[pl.ds(g * high * BLK, high * BLK)], out_sem.at[g]
            )
            write.start()
            writes.append(write)
    for write in writes[-panels:]:
        write.wait()


def densify(tables, blocks, rows, cols, *earlier):
    mats = len(blocks)
    slots = blocks[0].shape[0]
    panels = 4 if rows % 4 == 0 else 1
    shape = jax.ShapeDtypeStruct((rows * BLK, cols * BLK), jnp.bfloat16)
    return pl.pallas_call(
        functools.partial(densify_kernel, mats, rows, cols, panels),
        out_shape=(shape,) * mats,
        in_specs=[whole(SM)] * mats + [whole(pl.ANY)] * (mats + len(earlier)),
        out_specs=(whole(pl.ANY),) * mats,
        scratch_shapes=[
            VM((mats, slots + 1, BLK, BLK), jnp.bfloat16),
            VM((panels, rows // panels * BLK, cols * BLK), jnp.bfloat16),
            pltpu.SemaphoreType.DMA((mats,)),
            pltpu.SemaphoreType.DMA((panels,)),
        ],
        compiler_params=params(),
        cost_estimate=cost(0, mats * (slots + rows * cols) * BLK * BLK * 2),
    )(*tables, *blocks, *earlier)


def stream(copies, first):
    for copy in first:
        copy.start()
    copies[0].start()
    for copy in first:
        copy.wait()
    for n, copy in enumerate(copies):
        if n == 0:
            for ahead in copies[1:AHEAD]:
                ahead.start()
        copy.wait()
        if n + AHEAD < len(copies):
            copies[n + AHEAD].start()
        yield n


def product(panel, held, transposed):
    dims = (((1,), (1 if transposed else 0,)), ((), ()))
    return lax.dot_general(panel, held[...], dims, preferred_element_type=jnp.float32)


def project_kernel(transposed, tile, core_ref, panel, weight, *refs):
    mine_ref, other_ref = refs[-5:-3]
    held_panel, store, sem = refs[-3:]
    load = pltpu.make_async_copy(panel, held_panel, sem.at[0])
    is_first = core_ref[0] == 0
    half = panel.shape[0] // 2
    spans = [pl.ds(i * tile, tile) for i in range(mine_ref.shape[1] // tile)]
    places = [(at,) if transposed else (slice(None), at) for at in spans]
    copies = [
        pltpu.make_async_copy(weight.at[at], store.at[at], sem.at[1 + i])
        for i, at in enumerate(places)
    ]
    for i in stream(copies, [load]):
        full = product(held_panel[...], store.at[places[i]], transposed)
        first, second = full[:half], full[half:]
        mine_ref[:, spans[i]] = jnp.where(is_first, first, second)
        other_ref[:, spans[i]] = jnp.where(is_first, second, first).astype(jnp.bfloat16)


def project(core, panel, weight, transposed, *earlier):
    tokens, depth = panel.shape
    width = weight.shape[0] if transposed else weight.shape[1]
    tile = tile_of(width, PROJECT_TILE)
    shape = (tokens // 2, width)
    return pl.pallas_call(
        functools.partial(project_kernel, transposed, tile),
        out_shape=(
            jax.ShapeDtypeStruct(shape, jnp.float32),
            jax.ShapeDtypeStruct(shape, jnp.bfloat16),
        ),
        in_specs=[whole(SM)] + [whole(pl.ANY)] * (2 + len(earlier)),
        out_specs=(whole(VM),) * 2,
        scratch_shapes=[
            VM(panel.shape, jnp.bfloat16),
            VM(weight.shape, jnp.bfloat16),
            pltpu.SemaphoreType.DMA((1 + width // tile,)),
        ],
        compiler_params=params(),
        cost_estimate=cost(2 * tokens * depth * width, 2 * depth * width),
    )(core, panel, weight, *earlier)


def project_blocks_kernel(transposed, rows, cols, high, ring, core_ref, table, panel, blocks, *refs):
    mine_ref, other_ref, dense = refs[-8:-5]
    store, panel_ref, stage, in_sem, out_sem = refs[-5:]
    slots = blocks.shape[0]
    load = pltpu.make_async_copy(blocks, store.at[pl.ds(0, slots)], in_sem.at[0])
    load.start()
    load_panel = pltpu.make_async_copy(panel, panel_ref, in_sem.at[1])
    load_panel.start()
    store[slots] = jnp.zeros((BLK, BLK), jnp.bfloat16)
    is_first = core_ref[0] == 0
    half = panel_ref.shape[0] // 2
    load.wait()
    load_panel.wait()
    writes = []
    for i in range((rows if transposed else cols) // high):
        held = stage.at[i % ring]
        if i >= ring:
            writes[i - ring].wait()
        for far in range(cols if transposed else rows):
            for near in range(high):
                r, c = (i * high + near, far) if transposed else (far, i * high + near)
                r_at, c_at = (near, far) if transposed else (far, near)
                held[r_at * BLK : (r_at + 1) * BLK, c_at * BLK : (c_at + 1) * BLK] = store[
                    table[r * cols + c]
                ]
        at = pl.ds(i * high * BLK, high * BLK)
        write = pltpu.make_async_copy(
            held, dense.at[at] if transposed else dense.at[:, at], out_sem.at[i % ring]
        )
        write.start()
        writes.append(write)
        full = product(panel_ref[...], held, transposed)
        first, second = full[:half], full[half:]
        mine_ref[:, at] = jnp.where(is_first, first, second)
        other_ref[:, at] = jnp.where(is_first, second, first).astype(jnp.bfloat16)
    for write in writes[-ring:]:
        write.wait()


def project_blocks(core, panel, table, blocks, rows, cols, transposed, *earlier):
    tokens, _ = panel.shape
    slots = blocks.shape[0]
    cut, across = (rows, cols) if transposed else (cols, rows)
    high = tile_of(cut * BLK, 512) // BLK
    ring = min(3, cut // high)
    tile_shape = (high * BLK, across * BLK) if transposed else (across * BLK, high * BLK)
    shape = (tokens // 2, cut * BLK)
    return pl.pallas_call(
        functools.partial(project_blocks_kernel, transposed, rows, cols, high, ring),
        out_shape=(
            jax.ShapeDtypeStruct(shape, jnp.float32),
            jax.ShapeDtypeStruct(shape, jnp.bfloat16),
            jax.ShapeDtypeStruct((rows * BLK, cols * BLK), jnp.bfloat16),
        ),
        in_specs=[whole(SM)] * 2 + [whole(pl.ANY)] * (2 + len(earlier)),
        out_specs=(whole(VM), whole(VM), whole(pl.ANY)),
        scratch_shapes=[
            VM((slots + 1, BLK, BLK), jnp.bfloat16),
            VM(panel.shape, jnp.bfloat16),
            VM((ring, *tile_shape), jnp.bfloat16),
            pltpu.SemaphoreType.DMA((2,)),
            pltpu.SemaphoreType.DMA((ring,)),
        ],
        compiler_params=params(),
        cost_estimate=cost(2 * tokens * rows * cols * BLK * BLK, rows * cols * BLK * BLK * 4),
    )(core, table, panel, blocks, *earlier)


def back_kernel(transposed, n_pieces, mats, chunks, tile, core_ref, *refs):
    pieces, weights = refs[:n_pieces], refs[n_pieces : n_pieces + mats]
    outs = refs[-4 - chunks : -4]
    store, panel, sem, piece_sem = refs[-4:]
    half, depth = pieces[0].shape[1:]
    loads = [
        pltpu.make_async_copy(
            piece.at[w],
            panel.at[pl.ds(k * half, half), pl.ds(w * depth, depth)],
            piece_sem.at[w * n_pieces + k],
        )
        for w in range(mats)
        for k, piece in enumerate(pieces)
    ]
    is_first = core_ref[0] == 0
    rows = n_pieces * half // chunks
    copies = []
    for i in range(outs[0].shape[1] // tile):
        at = pl.ds(i * tile, tile)
        for w, weight in enumerate(weights):
            deep = pl.ds(w * depth, depth)
            source = weight.at[at] if transposed else weight.at[:, at]
            target = store.at[at, deep] if transposed else store.at[deep, at]
            copies.append(pltpu.make_async_copy(source, target, sem.at[w, i]))
    for n in stream(copies, loads):
        if n % mats < mats - 1:
            continue
        at = pl.ds(n // mats * tile, tile)
        total = product(panel[...], store.at[at] if transposed else store.at[:, at], transposed)
        mine, other = total[:half], total[half:]
        ordered = (jnp.where(is_first, mine, other), jnp.where(is_first, other, mine))
        for d in range(chunks):
            which, start = divmod(d * rows, half)
            outs[d][:, at] = ordered[which][start : start + rows].astype(outs[d].dtype)


def back(core, pieces, weights, chunks, transposed, *earlier):
    n_pieces, mats = len(pieces), len(weights)
    half, depth = pieces[0].shape[1:]
    width = weights[0].shape[0] if transposed else weights[0].shape[1]
    tile = tile_of(width, BACK_TILE)
    rows = n_pieces * half // chunks
    shapes = tuple(
        jax.ShapeDtypeStruct((rows, width), jnp.bfloat16 if d else jnp.float32)
        for d in range(chunks)
    )
    return pl.pallas_call(
        functools.partial(back_kernel, transposed, n_pieces, mats, chunks, tile),
        out_shape=shapes,
        in_specs=[whole(SM)] + [whole(pl.ANY)] * (n_pieces + mats + len(earlier)),
        out_specs=(whole(VM),) * chunks,
        scratch_shapes=[
            VM((width, mats * depth) if transposed else (mats * depth, width), jnp.bfloat16),
            VM((n_pieces * half, mats * depth), jnp.bfloat16),
            pltpu.SemaphoreType.DMA((mats, width // tile)),
            pltpu.SemaphoreType.DMA((mats * n_pieces,)),
        ],
        compiler_params=params(),
        cost_estimate=cost(
            2 * n_pieces * half * depth * width * mats, 2 * depth * width * mats
        ),
    )(core, *pieces, *weights, *earlier)


def pair_sum(mine, other, token=None):
    total = mine + other.astype(jnp.float32)
    if token is not None:
        total = total + token
    return total.astype(jnp.bfloat16)


def hold_kernel(*refs):
    del refs


def hold(x, *earlier):
    return pl.pallas_call(
        hold_kernel,
        out_shape=jax.ShapeDtypeStruct(x.shape, x.dtype),
        in_specs=[whole(pl.ANY)] * (1 + len(earlier)),
        out_specs=whole(pl.ANY),
        input_output_aliases={0: 0},
        compiler_params=params(),
        cost_estimate=pl.CostEstimate(flops=0, bytes_accessed=MARK, transcendentals=0),
    )(x, *earlier)


def sum_kernel(counts, *refs):
    at = 0
    for out, count in zip(refs[len(refs) - len(counts) :], counts):
        out[...] = add_up([ref[...] for ref in refs[at : at + count]]).astype(out.dtype)
        at += count


def sum_chunks(lists, *earlier):
    counts = [len(parts) for parts in lists]
    parts = [part for parts in lists for part in parts]
    return pl.pallas_call(
        functools.partial(sum_kernel, counts),
        out_shape=tuple(jax.ShapeDtypeStruct(p[0].shape, jnp.bfloat16) for p in lists),
        in_specs=[whole(VM)] * len(parts) + [whole(pl.ANY)] * len(earlier),
        out_specs=(whole(VM),) * len(lists),
        compiler_params=params(),
        cost_estimate=cost(0, parts[0].size * 10),
    )(*parts, *earlier)


def mark(*earlier):
    total = 0.0
    for x in earlier:
        corner = lax.slice(x, (0,) * x.ndim, (1,) * x.ndim).reshape(())
        total = total + jnp.abs(corner.astype(jnp.float32))
    return lax.optimization_barrier(jnp.minimum(total, 0.0))


def across(rows, width):
    return pl.BlockSpec((rows, tile_of(width, POINT_WIDE)), lambda i: (0, i))


def act_kernel(n_sum, *refs):
    gates, ups = refs[:n_sum], refs[n_sum : 2 * n_sum]
    hidden_ref, by_gate_ref, by_up_ref = refs[-3:]
    span = slice(None)
    gate = add_up([ref[:, span] for ref in gates])
    up = add_up([ref[:, span] for ref in ups])
    sigma = jax.nn.sigmoid(gate)
    active = gate * sigma
    hidden_ref[0, :, span] = (active * up).astype(jnp.bfloat16)
    by_gate_ref[:, span] = up * sigma * (1.0 + gate * (1.0 - sigma))
    by_up_ref[:, span] = active


def act(gates, ups, *earlier):
    rows, width = gates[0].shape
    wide = jax.ShapeDtypeStruct((rows, width), jnp.float32)
    return pl.pallas_call(
        functools.partial(act_kernel, len(gates)),
        out_shape=(jax.ShapeDtypeStruct((1, rows, width), jnp.bfloat16), wide, wide),
        grid=(width // tile_of(width, POINT_WIDE),),
        in_specs=[across(rows, width)] * (2 * len(gates)) + [whole(pl.ANY)] * len(earlier),
        out_specs=(
            pl.BlockSpec((1, rows, tile_of(width, POINT_WIDE)), lambda i: (0, 0, i)),
            across(rows, width),
            across(rows, width),
        ),
        compiler_params=params(),
        cost_estimate=cost(0, rows * width * 30),
    )(*gates, *ups, *earlier)


def grads_kernel(n_sum, *refs):
    sums, (by_gate_ref, by_up_ref) = refs[:n_sum], refs[n_sum : n_sum + 2]
    both_ref = refs[-1]
    span = slice(None)
    grad_hidden = add_up([ref[:, span] for ref in sums])
    both_ref[0, :, span] = (grad_hidden * by_gate_ref[:, span]).astype(jnp.bfloat16)
    both_ref[1, :, span] = (grad_hidden * by_up_ref[:, span]).astype(jnp.bfloat16)


def act_grads(sums, by_gate, by_up, *earlier):
    return pl.pallas_call(
        functools.partial(grads_kernel, len(sums)),
        out_shape=jax.ShapeDtypeStruct((2, *by_gate.shape), jnp.bfloat16),
        grid=(by_gate.shape[1] // tile_of(by_gate.shape[1], POINT_WIDE),),
        in_specs=[across(*by_gate.shape)] * (len(sums) + 2) + [whole(pl.ANY)] * len(earlier),
        out_specs=pl.BlockSpec(
            (2, by_gate.shape[0], tile_of(by_gate.shape[1], POINT_WIDE)), lambda i: (0, 0, i)
        ),
        compiler_params=params(),
        cost_estimate=cost(0, by_gate.size * 20),
    )(*sums, by_gate, by_up, *earlier)


def own_order(core, ref):
    half = ref.shape[0] // 2
    return [ref.at[rows_at(core * half, half)], ref.at[rows_at((1 - core) * half, half)]]


def block_grad_kernel(mats, n_left, n_right, scale, cols, wide, core_ref, *refs):
    tables, counts = refs[:mats], refs[mats : 2 * mats]
    lefts = refs[2 * mats : 2 * mats + n_left]
    rights = refs[2 * mats + n_left : 2 * mats + n_left + n_right]
    outs, stores = refs[-6 - 2 * mats : -6 - mats], refs[-6 - mats : -6]
    left, right, turned, in_sem, left_sem, out_sem = refs[-6:]
    core = core_ref[0]
    slots = outs[0].shape[0]
    length, width = left.shape[1], right.shape[2]
    tall = tile_of(length, 512)

    def rows_of(refs, m):
        rows = []
        for ref in refs:
            rows += own_order(core, ref) if len(ref.shape) == 2 else [ref.at[m]]
        return rows

    def loads(sources, target, sem):
        rows = sources[0].shape[0]
        copies = [
            pltpu.make_async_copy(source, target.at[pl.ds(k * rows, rows)], sem.at[k])
            for k, source in enumerate(sources)
        ]
        return copies

    left_loads = loads(rows_of(lefts, 0), left, left_sem)
    right_loads = [loads(rows_of(rights, m), right.at[m], in_sem.at[m]) for m in range(mats)]
    for load in left_loads:
        load.start()

    def clear(slot, carry, m):
        stores[m][slot] = jnp.zeros((BLK, BLK), jnp.bfloat16)
        return carry

    for m in range(mats):
        lax.fori_loop(counts[m][0], slots, functools.partial(clear, m=m), 0)
    for load in left_loads:
        load.wait()
    for load in right_loads[0]:
        load.start()
    for a in range(length // tall):
        span = slice(a * tall, (a + 1) * tall)
        turned[span, :] = left[:, span].T

    copies = []
    for m in range(mats):
        for load in right_loads[m]:
            load.wait()
        if m + 1 < mats:
            for load in right_loads[m + 1]:
                load.start()

        def column(at, carry, m=m):
            span = pl.ds(pl.multiple_of(at * wide, wide), wide)
            for a in range(length // tall):
                full = jnp.dot(
                    turned[a * tall : (a + 1) * tall, :],
                    right[m, :, span],
                    preferred_element_type=jnp.float32,
                )
                full = (full * scale).astype(jnp.bfloat16)
                for di in range(tall // BLK):
                    for dj in range(wide // BLK):
                        row = a * (tall // BLK) + di
                        slot = tables[m][row * cols + at * (wide // BLK) + dj]
                        stores[m][slot] = full[
                            di * BLK : (di + 1) * BLK, dj * BLK : (dj + 1) * BLK
                        ]
            return carry

        lax.fori_loop(0, width // wide, column, 0)
        copies.append(
            pltpu.make_async_copy(stores[m].at[pl.ds(0, slots)], outs[m], out_sem.at[m])
        )
        copies[m].start()
    for copy in copies:
        copy.wait()


def block_grads(core, tables, counts, lefts, rights, slots, scale, *earlier):
    mats = len(tables)
    tokens = sum(a.shape[-2] for a in lefts)
    length, width = lefts[0].shape[-1], rights[0].shape[-1]
    wide = tile_of(width, GRAD_WIDE)
    n_rows = [sum(2 if a.ndim == 2 else 1 for a in side) for side in (lefts, rights)]
    return pl.pallas_call(
        functools.partial(
            block_grad_kernel,
            mats,
            len(lefts),
            len(rights),
            scale,
            width // BLK,
            wide,
        ),
        out_shape=(jax.ShapeDtypeStruct((slots, BLK, BLK), jnp.bfloat16),) * mats,
        in_specs=[whole(SM)] * (1 + 2 * mats)
        + [whole(pl.ANY)] * (len(lefts) + len(rights) + len(earlier)),
        out_specs=(whole(pl.ANY),) * mats,
        scratch_shapes=[VM((slots + 1, BLK, BLK), jnp.bfloat16)] * mats
        + [
            VM((tokens, length), jnp.bfloat16),
            VM((mats, tokens, width), jnp.bfloat16),
            VM((length, tokens), jnp.bfloat16),
            pltpu.SemaphoreType.DMA((mats, n_rows[1])),
            pltpu.SemaphoreType.DMA((n_rows[0],)),
            pltpu.SemaphoreType.DMA((mats,)),
        ],
        compiler_params=params(),
        cost_estimate=cost(2 * tokens * length * width * mats, slots * BLK * BLK * 2 * mats),
    )(core, *tables, *counts, *lefts, *rights, *earlier)


def shift(x, axis, by):
    n = lax.axis_size(axis)
    return lax.ppermute(x, axis, [(i, (i + by) % n) for i in range(n)])


def swap_cores(x):
    n = lax.axis_size("row")
    return lax.ppermute(x, "row", [(i, i ^ 1) for i in range(n)])


def add_up(parts):
    total = parts[0].astype(jnp.float32)
    for part in parts[1:]:
        total = total + part.astype(jnp.float32)
    return total


def z_order(n):
    return sorted(range(1, n), key=lambda d: (min(d, n - d), d))


def other_chips(sent):
    n = lax.axis_size("row")
    return [shift(sent, "row", 2 * s) for s in range(1, n // 2)]


def other_groups(x):
    return [shift(x, "dp", s) for s in range(1, lax.axis_size("dp"))]


def on_device(
    tokens, cotangent, gate_blocks, gate_index, up_blocks, up_index, down_blocks, down_index
):
    n_col = lax.axis_size("col")
    parts = 1
    chunks = n_col // parts
    core = lax.rem(lax.axis_index("row"), 2).astype(jnp.int32).reshape(1)
    feats = tokens.shape[1] // BLK
    units = FF // BLK // n_col
    width = units * BLK
    slots = gate_blocks.shape[2]
    group_rows = tokens.shape[0] * n_col
    scale = 1.0 / math.sqrt(group_rows * lax.axis_size("dp"))

    def gather(x):
        got = {0: x}
        for d in z_order(n_col):
            got[d] = shift(x, "col", d)
        return [
            jnp.concatenate([got[d] for d in range(p * chunks, (p + 1) * chunks)], axis=0)
            for p in range(parts)
        ]

    def scatter(cut):
        return [cut[0]] + [shift(cut[d], "col", -d) for d in z_order(n_col)]

    def far_pieces(pairs):
        pieces = []
        for s in range(lax.axis_size("dp") - 1):
            for far in pairs:
                pieces += [far[s], swap_cores(far[s])]
        return pieces

    gate_table, gate_count = slot_table(gate_index, feats, units)
    up_table, up_count = slot_table(up_index, feats, units)
    down_table, down_count = slot_table(down_index, units, feats)

    x_parts = gather(tokens)
    x_whole = jnp.concatenate(x_parts, axis=0)
    (w_gate,) = densify((gate_table,), (gate_blocks[0, 0],), feats, units)
    gate_mine, gate_other = project(core, x_whole, w_gate, False)
    gate_swapped = swap_cores(gate_other)
    gate_sent = pair_sum(gate_mine, gate_swapped)

    gate_got = other_chips(gate_sent)
    c_parts = gather(after(cotangent, x_whole))
    c_whole = jnp.concatenate(c_parts, axis=0)
    x_groups = [x_whole] + other_groups(x_whole)
    up_mine, up_other, w_up = project_blocks(
        core, x_whole, up_table, up_blocks[0, 0], feats, units, False, gate_sent
    )
    token = mark(*gate_got, c_whole, *x_groups[1:])
    up_swapped = swap_cores(up_other)
    up_sent = pair_sum(up_mine, up_swapped, token)

    up_got = other_chips(up_sent)
    c_groups = [c_whole] + other_groups(c_whole)
    back_mine, back_other, w_down = project_blocks(
        core, c_whole, down_table, down_blocks[0, 0], units, feats, True, up_sent
    )
    token = mark(*up_got, *c_groups[1:])
    back_swapped = swap_cores(back_other)
    back_sent = pair_sum(back_mine, back_swapped, token)

    back_got = other_chips(back_sent)
    hidden, by_gate, by_up = act(
        [gate_mine, gate_swapped] + gate_got, [up_mine, up_swapped] + up_got, back_sent
    )
    hidden_far = other_groups(hidden)
    hidden_pieces = [hidden, swap_cores(hidden)]
    out_cut = back(core, hidden_pieces, [w_down], n_col, False)
    grads = act_grads([back_mine, back_swapped] + back_got, by_gate, by_up, out_cut[0])
    hidden_pieces += far_pieces([[hold(far, grads) for far in hidden_far]])

    grads_far = other_groups(grads)
    grad_pieces = [grads, swap_cores(grads)]
    (down_grad,) = block_grads(
        core,
        (down_table,),
        (down_count,),
        hidden_pieces,
        c_groups,
        slots,
        scale,
        grads,
    )
    in_cut = back(core, grad_pieces, [w_gate, w_up], n_col, True, down_grad)
    out_kept = scatter(out_cut)
    grads_far = [hold(far, in_cut[0], *out_kept[1:]) for far in grads_far]
    gate_grad, up_grad = block_grads(
        core,
        (gate_table, up_table),
        (gate_count, up_count),
        x_groups,
        grad_pieces + far_pieces([grads_far]),
        slots,
        scale,
    )
    output, input_grad = sum_chunks([out_kept, scatter(in_cut)], gate_grad)
    shape = gate_blocks.shape
    return (
        output,
        input_grad,
        gate_grad.reshape(shape),
        up_grad.reshape(shape),
        down_grad.reshape(shape),
    )


def solution(mesh):
    return jax.shard_map(
        on_device,
        mesh=mesh,
        in_specs=(
            P(("dp", "col"), "row"),
            P(("dp", "col"), "row"),
            P("row", "col", None, None, None),
            P("row", "col", None, None),
            P("row", "col", None, None, None),
            P("row", "col", None, None),
            P("row", "col", None, None, None),
            P("row", "col", None, None),
        ),
        out_specs=(
            P(("dp", "col"), "row"),
            P(("dp", "col"), "row"),
            P("row", "col", None, None, None),
            P("row", "col", None, None, None),
            P("row", "col", None, None, None),
        ),
        check_vma=False,
    )
```

```python
import functools
import math

import jax
import jax.numpy as jnp
from jax import lax
from jax.experimental import pallas as pl
from jax.experimental.pallas import tpu as pltpu
from jax.sharding import PartitionSpec as P

BLK = 128
AHEAD = 3
PROJECT_TILE = 512
BACK_TILE = 512
GRAD_WIDE = 512
POINT_WIDE = 1792
COST = 0.000001
MARK = 200000
FF = 14336
VMEM_LIMIT = 56 * 1024 * 1024
VM = pltpu.VMEM
SM = pltpu.SMEM


def params():
    return pltpu.CompilerParams(vmem_limit_bytes=VMEM_LIMIT)


def cost(flops, nbytes):
    return pl.CostEstimate(
        flops=int(flops * COST), bytes_accessed=int(nbytes * COST), transcendentals=0
    )


def tile_of(size, largest):
    return max(t for t in range(BLK, largest + 1, BLK) if size % t == 0)


def rows_at(start, rows):
    return pl.ds(pl.multiple_of(start, rows), rows)


def whole(memory_space):
    return pl.BlockSpec(memory_space=memory_space)


def after(x, *earlier):
    return lax.optimization_barrier((x, *earlier))[0]


def slot_table(index_list, first_count, second_count):
    listing = index_list[0, 0]
    slots = listing.shape[0]
    flat = jnp.where(listing[:, 0] >= 0, listing[:, 0] * second_count + listing[:, 1], -1)
    positions = jnp.arange(first_count * second_count, dtype=jnp.int32)
    hits = flat[None, :] == positions[:, None]
    back_from = slots - jnp.arange(slots, dtype=jnp.int32)
    table = slots - jnp.sum(jnp.where(hits, back_from[None, :], 0), axis=1)
    count = jnp.sum((flat >= 0).astype(jnp.int32))
    return table, count.reshape(1)


def densify_kernel(mats, rows, cols, panels, *refs):
    tables, blocks = refs[:mats], refs[mats : 2 * mats]
    outs = refs[-4 - mats : -4]
    store, stage, in_sem, out_sem = refs[-4:]
    slots = blocks[0].shape[0]
    loads = [
        pltpu.make_async_copy(blocks[m], store.at[m, pl.ds(0, slots)], in_sem.at[m])
        for m in range(mats)
    ]
    for load in loads:
        load.start()
    high = rows // panels
    writes = []
    for m in range(mats):
        store[m, slots] = jnp.zeros((BLK, BLK), jnp.bfloat16)
        loads[m].wait()
        for g in range(panels):
            if m:
                writes[(m - 1) * panels + g].wait()

            def fill(r, carry, m=m, g=g):
                for j in range(cols):
                    slot = tables[m][(g * high + r) * cols + j]
                    stage[g, rows_at(r * BLK, BLK), j * BLK : (j + 1) * BLK] = store[m, slot]
                return carry

            lax.fori_loop(0, high, fill, 0)
            write = pltpu.make_async_copy(
                stage.at[g], outs[m].at[pl.ds(g * high * BLK, high * BLK)], out_sem.at[g]
            )
            write.start()
            writes.append(write)
    for write in writes[-panels:]:
        write.wait()


def densify(tables, blocks, rows, cols, *earlier):
    mats = len(blocks)
    slots = blocks[0].shape[0]
    panels = 4 if rows % 4 == 0 else 1
    shape = jax.ShapeDtypeStruct((rows * BLK, cols * BLK), jnp.bfloat16)
    return pl.pallas_call(
        functools.partial(densify_kernel, mats, rows, cols, panels),
        out_shape=(shape,) * mats,
        in_specs=[whole(SM)] * mats + [whole(pl.ANY)] * (mats + len(earlier)),
        out_specs=(whole(pl.ANY),) * mats,
        scratch_shapes=[
            VM((mats, slots + 1, BLK, BLK), jnp.bfloat16),
            VM((panels, rows // panels * BLK, cols * BLK), jnp.bfloat16),
            pltpu.SemaphoreType.DMA((mats,)),
            pltpu.SemaphoreType.DMA((panels,)),
        ],
        compiler_params=params(),
        cost_estimate=cost(0, mats * (slots + rows * cols) * BLK * BLK * 2),
    )(*tables, *blocks, *earlier)


def stream(copies, first):
    for copy in first:
        copy.start()
    copies[0].start()
    for copy in first:
        copy.wait()
    for n, copy in enumerate(copies):
        if n == 0:
            for ahead in copies[1:AHEAD]:
                ahead.start()
        copy.wait()
        if n + AHEAD < len(copies):
            copies[n + AHEAD].start()
        yield n


def product(panel, held, transposed):
    dims = (((1,), (1 if transposed else 0,)), ((), ()))
    return lax.dot_general(panel, held[...], dims, preferred_element_type=jnp.float32)


def project_kernel(transposed, tile, core_ref, panel, weight, *refs):
    mine_ref, other_ref = refs[-5:-3]
    held_panel, store, sem = refs[-3:]
    load = pltpu.make_async_copy(panel, held_panel, sem.at[0])
    is_first = core_ref[0] == 0
    half = panel.shape[0] // 2
    spans = [pl.ds(i * tile, tile) for i in range(mine_ref.shape[1] // tile)]
    places = [(at,) if transposed else (slice(None), at) for at in spans]
    copies = [
        pltpu.make_async_copy(weight.at[at], store.at[at], sem.at[1 + i])
        for i, at in enumerate(places)
    ]
    for i in stream(copies, [load]):
        full = product(held_panel[...], store.at[places[i]], transposed)
        first, second = full[:half], full[half:]
        mine_ref[:, spans[i]] = jnp.where(is_first, first, second)
        other_ref[:, spans[i]] = jnp.where(is_first, second, first).astype(jnp.bfloat16)


def project(core, panel, weight, transposed, *earlier):
    tokens, depth = panel.shape
    width = weight.shape[0] if transposed else weight.shape[1]
    tile = tile_of(width, PROJECT_TILE)
    shape = (tokens // 2, width)
    return pl.pallas_call(
        functools.partial(project_kernel, transposed, tile),
        out_shape=(
            jax.ShapeDtypeStruct(shape, jnp.float32),
            jax.ShapeDtypeStruct(shape, jnp.bfloat16),
        ),
        in_specs=[whole(SM)] + [whole(pl.ANY)] * (2 + len(earlier)),
        out_specs=(whole(VM),) * 2,
        scratch_shapes=[
            VM(panel.shape, jnp.bfloat16),
            VM(weight.shape, jnp.bfloat16),
            pltpu.SemaphoreType.DMA((1 + width // tile,)),
        ],
        compiler_params=params(),
        cost_estimate=cost(2 * tokens * depth * width, 2 * depth * width),
    )(core, panel, weight, *earlier)


def project_blocks_kernel(transposed, rows, cols, high, ring, core_ref, table, panel, blocks, *refs):
    mine_ref, other_ref, dense = refs[-8:-5]
    store, panel_ref, stage, in_sem, out_sem = refs[-5:]
    slots = blocks.shape[0]
    load = pltpu.make_async_copy(blocks, store.at[pl.ds(0, slots)], in_sem.at[0])
    load.start()
    load_panel = pltpu.make_async_copy(panel, panel_ref, in_sem.at[1])
    load_panel.start()
    store[slots] = jnp.zeros((BLK, BLK), jnp.bfloat16)
    is_first = core_ref[0] == 0
    half = panel_ref.shape[0] // 2
    load.wait()
    load_panel.wait()
    writes = []
    for i in range((rows if transposed else cols) // high):
        held = stage.at[i % ring]
        if i >= ring:
            writes[i - ring].wait()
        for far in range(cols if transposed else rows):
            for near in range(high):
                r, c = (i * high + near, far) if transposed else (far, i * high + near)
                r_at, c_at = (near, far) if transposed else (far, near)
                held[r_at * BLK : (r_at + 1) * BLK, c_at * BLK : (c_at + 1) * BLK] = store[
                    table[r * cols + c]
                ]
        at = pl.ds(i * high * BLK, high * BLK)
        write = pltpu.make_async_copy(
            held, dense.at[at] if transposed else dense.at[:, at], out_sem.at[i % ring]
        )
        write.start()
        writes.append(write)
        full = product(panel_ref[...], held, transposed)
        first, second = full[:half], full[half:]
        mine_ref[:, at] = jnp.where(is_first, first, second)
        other_ref[:, at] = jnp.where(is_first, second, first).astype(jnp.bfloat16)
    for write in writes[-ring:]:
        write.wait()


def project_blocks(core, panel, table, blocks, rows, cols, transposed, *earlier):
    tokens, _ = panel.shape
    slots = blocks.shape[0]
    cut, across = (rows, cols) if transposed else (cols, rows)
    high = tile_of(cut * BLK, 512) // BLK
    ring = min(3, cut // high)
    tile_shape = (high * BLK, across * BLK) if transposed else (across * BLK, high * BLK)
    shape = (tokens // 2, cut * BLK)
    return pl.pallas_call(
        functools.partial(project_blocks_kernel, transposed, rows, cols, high, ring),
        out_shape=(
            jax.ShapeDtypeStruct(shape, jnp.float32),
            jax.ShapeDtypeStruct(shape, jnp.bfloat16),
            jax.ShapeDtypeStruct((rows * BLK, cols * BLK), jnp.bfloat16),
        ),
        in_specs=[whole(SM)] * 2 + [whole(pl.ANY)] * (2 + len(earlier)),
        out_specs=(whole(VM), whole(VM), whole(pl.ANY)),
        scratch_shapes=[
            VM((slots + 1, BLK, BLK), jnp.bfloat16),
            VM(panel.shape, jnp.bfloat16),
            VM((ring, *tile_shape), jnp.bfloat16),
            pltpu.SemaphoreType.DMA((2,)),
            pltpu.SemaphoreType.DMA((ring,)),
        ],
        compiler_params=params(),
        cost_estimate=cost(2 * tokens * rows * cols * BLK * BLK, rows * cols * BLK * BLK * 4),
    )(core, table, panel, blocks, *earlier)


def back_kernel(transposed, n_pieces, mats, chunks, tile, core_ref, *refs):
    pieces, weights = refs[:n_pieces], refs[n_pieces : n_pieces + mats]
    outs = refs[-4 - chunks : -4]
    store, panel, sem, piece_sem = refs[-4:]
    half, depth = pieces[0].shape[1:]
    loads = [
        pltpu.make_async_copy(
            piece.at[w],
            panel.at[pl.ds(k * half, half), pl.ds(w * depth, depth)],
            piece_sem.at[w * n_pieces + k],
        )
        for w in range(mats)
        for k, piece in enumerate(pieces)
    ]
    is_first = core_ref[0] == 0
    rows = n_pieces * half // chunks
    copies = []
    for i in range(outs[0].shape[1] // tile):
        at = pl.ds(i * tile, tile)
        for w, weight in enumerate(weights):
            deep = pl.ds(w * depth, depth)
            source = weight.at[at] if transposed else weight.at[:, at]
            target = store.at[at, deep] if transposed else store.at[deep, at]
            copies.append(pltpu.make_async_copy(source, target, sem.at[w, i]))
    for n in stream(copies, loads):
        if n % mats < mats - 1:
            continue
        at = pl.ds(n // mats * tile, tile)
        total = product(panel[...], store.at[at] if transposed else store.at[:, at], transposed)
        mine, other = total[:half], total[half:]
        ordered = (jnp.where(is_first, mine, other), jnp.where(is_first, other, mine))
        for d in range(chunks):
            which, start = divmod(d * rows, half)
            outs[d][:, at] = ordered[which][start : start + rows].astype(outs[d].dtype)


def back(core, pieces, weights, chunks, transposed, *earlier):
    n_pieces, mats = len(pieces), len(weights)
    half, depth = pieces[0].shape[1:]
    width = weights[0].shape[0] if transposed else weights[0].shape[1]
    tile = tile_of(width, BACK_TILE)
    rows = n_pieces * half // chunks
    shapes = tuple(
        jax.ShapeDtypeStruct((rows, width), jnp.bfloat16 if d else jnp.float32)
        for d in range(chunks)
    )
    return pl.pallas_call(
        functools.partial(back_kernel, transposed, n_pieces, mats, chunks, tile),
        out_shape=shapes,
        in_specs=[whole(SM)] + [whole(pl.ANY)] * (n_pieces + mats + len(earlier)),
        out_specs=(whole(VM),) * chunks,
        scratch_shapes=[
            VM((width, mats * depth) if transposed else (mats * depth, width), jnp.bfloat16),
            VM((n_pieces * half, mats * depth), jnp.bfloat16),
            pltpu.SemaphoreType.DMA((mats, width // tile)),
            pltpu.SemaphoreType.DMA((mats * n_pieces,)),
        ],
        compiler_params=params(),
        cost_estimate=cost(
            2 * n_pieces * half * depth * width * mats, 2 * depth * width * mats
        ),
    )(core, *pieces, *weights, *earlier)


def pair_sum(mine, other, token=None):
    total = mine + other.astype(jnp.float32)
    if token is not None:
        total = total + token
    return total.astype(jnp.bfloat16)


def hold_kernel(*refs):
    del refs


def hold(x, *earlier):
    return pl.pallas_call(
        hold_kernel,
        out_shape=jax.ShapeDtypeStruct(x.shape, x.dtype),
        in_specs=[whole(pl.ANY)] * (1 + len(earlier)),
        out_specs=whole(pl.ANY),
        input_output_aliases={0: 0},
        compiler_params=params(),
        cost_estimate=pl.CostEstimate(flops=0, bytes_accessed=MARK, transcendentals=0),
    )(x, *earlier)


def sum_kernel(counts, *refs):
    at = 0
    for out, count in zip(refs[len(refs) - len(counts) :], counts):
        out[...] = add_up([ref[...] for ref in refs[at : at + count]]).astype(out.dtype)
        at += count


def sum_chunks(lists, *earlier):
    counts = [len(parts) for parts in lists]
    parts = [part for parts in lists for part in parts]
    return pl.pallas_call(
        functools.partial(sum_kernel, counts),
        out_shape=tuple(jax.ShapeDtypeStruct(p[0].shape, jnp.bfloat16) for p in lists),
        in_specs=[whole(VM)] * len(parts) + [whole(pl.ANY)] * len(earlier),
        out_specs=(whole(VM),) * len(lists),
        compiler_params=params(),
        cost_estimate=cost(0, parts[0].size * 10),
    )(*parts, *earlier)


def mark(*earlier):
    total = 0.0
    for x in earlier:
        corner = lax.slice(x, (0,) * x.ndim, (1,) * x.ndim).reshape(())
        total = total + jnp.abs(corner.astype(jnp.float32))
    return lax.optimization_barrier(jnp.minimum(total, 0.0))


def across(rows, width):
    return pl.BlockSpec((rows, tile_of(width, POINT_WIDE)), lambda i: (0, i))


def hidden_kernel(n_sum, *refs):
    gate = add_up([ref[...] for ref in refs[:n_sum]])
    up = add_up([ref[...] for ref in refs[n_sum : 2 * n_sum]])
    refs[-1][0] = (gate * jax.nn.sigmoid(gate) * up).astype(jnp.bfloat16)


def slopes_kernel(n_sum, *refs):
    gate = add_up([ref[...] for ref in refs[:n_sum]])
    up = add_up([ref[...] for ref in refs[n_sum : 2 * n_sum]])
    sigma = jax.nn.sigmoid(gate)
    refs[-2][...] = up * sigma * (1.0 + gate * (1.0 - sigma))
    refs[-1][...] = gate * sigma


def pointwise(kernel, gates, ups, outs, *earlier):
    rows, width = gates[0].shape
    return pl.pallas_call(
        functools.partial(kernel, len(gates)),
        out_shape=tuple(shape for shape, _ in outs),
        grid=(width // tile_of(width, POINT_WIDE),),
        in_specs=[across(rows, width)] * (2 * len(gates)) + [whole(pl.ANY)] * len(earlier),
        out_specs=tuple(spec for _, spec in outs),
        compiler_params=params(),
        cost_estimate=cost(0, rows * width * 30),
    )(*gates, *ups, *earlier)


def act(gates, ups, *earlier):
    rows, width = gates[0].shape
    spec = pl.BlockSpec((1, rows, tile_of(width, POINT_WIDE)), lambda i: (0, 0, i))
    outs = [(jax.ShapeDtypeStruct((1, rows, width), jnp.bfloat16), spec)]
    return pointwise(hidden_kernel, gates, ups, outs, *earlier)[0]


def slopes(gates, ups, *earlier):
    rows, width = gates[0].shape
    out = (jax.ShapeDtypeStruct((rows, width), jnp.float32), across(rows, width))
    return pointwise(slopes_kernel, gates, ups, [out, out], *earlier)


def grads_kernel(n_sum, *refs):
    sums, (by_gate_ref, by_up_ref) = refs[:n_sum], refs[n_sum : n_sum + 2]
    both_ref = refs[-1]
    span = slice(None)
    grad_hidden = add_up([ref[:, span] for ref in sums])
    both_ref[0, :, span] = (grad_hidden * by_gate_ref[:, span]).astype(jnp.bfloat16)
    both_ref[1, :, span] = (grad_hidden * by_up_ref[:, span]).astype(jnp.bfloat16)


def act_grads(sums, by_gate, by_up, *earlier):
    return pl.pallas_call(
        functools.partial(grads_kernel, len(sums)),
        out_shape=jax.ShapeDtypeStruct((2, *by_gate.shape), jnp.bfloat16),
        grid=(by_gate.shape[1] // tile_of(by_gate.shape[1], POINT_WIDE),),
        in_specs=[across(*by_gate.shape)] * (len(sums) + 2) + [whole(pl.ANY)] * len(earlier),
        out_specs=pl.BlockSpec(
            (2, by_gate.shape[0], tile_of(by_gate.shape[1], POINT_WIDE)), lambda i: (0, 0, i)
        ),
        compiler_params=params(),
        cost_estimate=cost(0, by_gate.size * 20),
    )(*sums, by_gate, by_up, *earlier)


def own_order(core, ref):
    half = ref.shape[0] // 2
    return [ref.at[rows_at(core * half, half)], ref.at[rows_at((1 - core) * half, half)]]


def block_grad_kernel(mats, n_left, n_right, scale, cols, wide, core_ref, *refs):
    tables, counts = refs[:mats], refs[mats : 2 * mats]
    lefts = refs[2 * mats : 2 * mats + n_left]
    rights = refs[2 * mats + n_left : 2 * mats + n_left + n_right]
    outs, stores = refs[-6 - 2 * mats : -6 - mats], refs[-6 - mats : -6]
    left, right, turned, in_sem, left_sem, out_sem = refs[-6:]
    core = core_ref[0]
    slots = outs[0].shape[0]
    length, width = left.shape[1], right.shape[2]
    tall = tile_of(length, 512)

    def rows_of(refs, m):
        rows = []
        for ref in refs:
            rows += own_order(core, ref) if len(ref.shape) == 2 else [ref.at[m]]
        return rows

    def loads(sources, target, sem):
        rows = sources[0].shape[0]
        copies = [
            pltpu.make_async_copy(source, target.at[pl.ds(k * rows, rows)], sem.at[k])
            for k, source in enumerate(sources)
        ]
        return copies

    left_loads = loads(rows_of(lefts, 0), left, left_sem)
    right_loads = [loads(rows_of(rights, m), right.at[m], in_sem.at[m]) for m in range(mats)]
    for load in left_loads:
        load.start()

    def clear(slot, carry, m):
        stores[m][slot] = jnp.zeros((BLK, BLK), jnp.bfloat16)
        return carry

    for m in range(mats):
        lax.fori_loop(counts[m][0], slots, functools.partial(clear, m=m), 0)
    for load in left_loads:
        load.wait()
    for load in right_loads[0]:
        load.start()
    for a in range(length // tall):
        span = slice(a * tall, (a + 1) * tall)
        turned[span, :] = left[:, span].T

    copies = []
    for m in range(mats):
        for load in right_loads[m]:
            load.wait()
        if m + 1 < mats:
            for load in right_loads[m + 1]:
                load.start()

        def column(at, carry, m=m):
            span = pl.ds(pl.multiple_of(at * wide, wide), wide)
            for a in range(length // tall):
                full = jnp.dot(
                    turned[a * tall : (a + 1) * tall, :],
                    right[m, :, span],
                    preferred_element_type=jnp.float32,
                )
                full = (full * scale).astype(jnp.bfloat16)
                for di in range(tall // BLK):
                    for dj in range(wide // BLK):
                        row = a * (tall // BLK) + di
                        slot = tables[m][row * cols + at * (wide // BLK) + dj]
                        stores[m][slot] = full[
                            di * BLK : (di + 1) * BLK, dj * BLK : (dj + 1) * BLK
                        ]
            return carry

        lax.fori_loop(0, width // wide, column, 0)
        copies.append(
            pltpu.make_async_copy(stores[m].at[pl.ds(0, slots)], outs[m], out_sem.at[m])
        )
        copies[m].start()
    for copy in copies:
        copy.wait()


def block_grads(core, tables, counts, lefts, rights, slots, scale, *earlier):
    mats = len(tables)
    tokens = sum(a.shape[-2] for a in lefts)
    length, width = lefts[0].shape[-1], rights[0].shape[-1]
    wide = tile_of(width, GRAD_WIDE)
    n_rows = [sum(2 if a.ndim == 2 else 1 for a in side) for side in (lefts, rights)]
    return pl.pallas_call(
        functools.partial(
            block_grad_kernel,
            mats,
            len(lefts),
            len(rights),
            scale,
            width // BLK,
            wide,
        ),
        out_shape=(jax.ShapeDtypeStruct((slots, BLK, BLK), jnp.bfloat16),) * mats,
        in_specs=[whole(SM)] * (1 + 2 * mats)
        + [whole(pl.ANY)] * (len(lefts) + len(rights) + len(earlier)),
        out_specs=(whole(pl.ANY),) * mats,
        scratch_shapes=[VM((slots + 1, BLK, BLK), jnp.bfloat16)] * mats
        + [
            VM((tokens, length), jnp.bfloat16),
            VM((mats, tokens, width), jnp.bfloat16),
            VM((length, tokens), jnp.bfloat16),
            pltpu.SemaphoreType.DMA((mats, n_rows[1])),
            pltpu.SemaphoreType.DMA((n_rows[0],)),
            pltpu.SemaphoreType.DMA((mats,)),
        ],
        compiler_params=params(),
        cost_estimate=cost(2 * tokens * length * width * mats, slots * BLK * BLK * 2 * mats),
    )(core, *tables, *counts, *lefts, *rights, *earlier)


def shift(x, axis, by):
    n = lax.axis_size(axis)
    return lax.ppermute(x, axis, [(i, (i + by) % n) for i in range(n)])


def swap_cores(x):
    n = lax.axis_size("row")
    return lax.ppermute(x, "row", [(i, i ^ 1) for i in range(n)])


def add_up(parts):
    total = parts[0].astype(jnp.float32)
    for part in parts[1:]:
        total = total + part.astype(jnp.float32)
    return total


def z_order(n):
    return sorted(range(1, n), key=lambda d: (min(d, n - d), d))


def other_chips(sent):
    n = lax.axis_size("row")
    return [shift(sent, "row", 2 * s) for s in range(1, n // 2)]


def other_groups(x):
    return [shift(x, "dp", s) for s in range(1, lax.axis_size("dp"))]


def on_device(
    tokens, cotangent, gate_blocks, gate_index, up_blocks, up_index, down_blocks, down_index
):
    n_col = lax.axis_size("col")
    parts = 1
    chunks = n_col // parts
    core = lax.rem(lax.axis_index("row"), 2).astype(jnp.int32).reshape(1)
    feats = tokens.shape[1] // BLK
    units = FF // BLK // n_col
    width = units * BLK
    slots = gate_blocks.shape[2]
    group_rows = tokens.shape[0] * n_col
    scale = 1.0 / math.sqrt(group_rows * lax.axis_size("dp"))

    def gather(x):
        got = {0: x}
        for d in z_order(n_col):
            got[d] = shift(x, "col", d)
        return [
            jnp.concatenate([got[d] for d in range(p * chunks, (p + 1) * chunks)], axis=0)
            for p in range(parts)
        ]

    def scatter(cut):
        return [cut[0]] + [shift(cut[d], "col", -d) for d in z_order(n_col)]

    def far_pieces(pairs):
        pieces = []
        for s in range(lax.axis_size("dp") - 1):
            for far in pairs:
                pieces += [far[s], swap_cores(far[s])]
        return pieces

    gate_table, gate_count = slot_table(gate_index, feats, units)
    up_table, up_count = slot_table(up_index, feats, units)
    down_table, down_count = slot_table(down_index, units, feats)

    x_parts = gather(tokens)
    x_whole = jnp.concatenate(x_parts, axis=0)
    (w_gate,) = densify((gate_table,), (gate_blocks[0, 0],), feats, units)
    gate_mine, gate_other = project(core, x_whole, w_gate, False)
    gate_swapped = swap_cores(gate_other)
    gate_sent = pair_sum(gate_mine, gate_swapped)

    gate_got = other_chips(gate_sent)
    c_parts = gather(after(cotangent, x_whole))
    c_whole = jnp.concatenate(c_parts, axis=0)
    x_groups = [x_whole] + other_groups(x_whole)
    up_mine, up_other, w_up = project_blocks(
        core, x_whole, up_table, up_blocks[0, 0], feats, units, False, gate_sent
    )
    token = mark(*gate_got, c_whole, *x_groups[1:])
    up_swapped = swap_cores(up_other)
    up_sent = pair_sum(up_mine, up_swapped, token)

    up_got = other_chips(up_sent)
    c_groups = [c_whole] + other_groups(c_whole)
    back_mine, back_other, w_down = project_blocks(
        core, c_whole, down_table, down_blocks[0, 0], units, feats, True, up_sent
    )
    token = mark(*up_got, *c_groups[1:])
    back_swapped = swap_cores(back_other)
    back_sent = pair_sum(back_mine, back_swapped, token)

    back_got = other_chips(back_sent)
    gate_sums = [gate_mine, gate_swapped] + gate_got
    up_sums = [up_mine, up_swapped] + up_got
    hidden = act(gate_sums, up_sums, back_sent)
    hidden_far = other_groups(hidden)
    hidden_pieces = [hidden, swap_cores(hidden)]
    out_cut = back(core, hidden_pieces, [w_down], n_col, False)
    by_gate, by_up = slopes(gate_sums, up_sums, out_cut[0])
    grads = act_grads([back_mine, back_swapped] + back_got, by_gate, by_up)
    hidden_pieces += far_pieces([[hold(far, grads) for far in hidden_far]])

    grads_far = other_groups(grads)
    grad_pieces = [grads, swap_cores(grads)]
    (down_grad,) = block_grads(
        core,
        (down_table,),
        (down_count,),
        hidden_pieces,
        c_groups,
        slots,
        scale,
        grads,
    )
    in_cut = back(core, grad_pieces, [w_gate, w_up], n_col, True, down_grad)
    out_kept = scatter(out_cut)
    grads_far = [hold(far, in_cut[0], *out_kept[1:]) for far in grads_far]
    gate_grad, up_grad = block_grads(
        core,
        (gate_table, up_table),
        (gate_count, up_count),
        x_groups,
        grad_pieces + far_pieces([grads_far]),
        slots,
        scale,
    )
    output, input_grad = sum_chunks([out_kept, scatter(in_cut)], gate_grad)
    shape = gate_blocks.shape
    return (
        output,
        input_grad,
        gate_grad.reshape(shape),
        up_grad.reshape(shape),
        down_grad.reshape(shape),
    )


def solution(mesh):
    return jax.shard_map(
        on_device,
        mesh=mesh,
        in_specs=(
            P(("dp", "col"), "row"),
            P(("dp", "col"), "row"),
            P("row", "col", None, None, None),
            P("row", "col", None, None),
            P("row", "col", None, None, None),
            P("row", "col", None, None),
            P("row", "col", None, None, None),
            P("row", "col", None, None),
        ),
        out_specs=(
            P(("dp", "col"), "row"),
            P(("dp", "col"), "row"),
            P("row", "col", None, None, None),
            P("row", "col", None, None, None),
            P("row", "col", None, None, None),
        ),
        check_vma=False,
    )
```

```python
import functools
import math

import jax
import jax.numpy as jnp
from jax import lax
from jax.experimental import pallas as pl
from jax.experimental.pallas import tpu as pltpu
from jax.sharding import PartitionSpec as P

BLK = 128
AHEAD = 3
PROJECT_TILE = 512
BACK_TILE = 512
GRAD_WIDE = 512
POINT_WIDE = 1792
COST = 0.000001
MARK = 200000
FF = 14336
VMEM_LIMIT = 56 * 1024 * 1024
VM = pltpu.VMEM
SM = pltpu.SMEM


def params():
    return pltpu.CompilerParams(vmem_limit_bytes=VMEM_LIMIT)


def cost(flops, nbytes):
    return pl.CostEstimate(
        flops=int(flops * COST), bytes_accessed=int(nbytes * COST), transcendentals=0
    )


def tile_of(size, largest):
    return max(t for t in range(BLK, largest + 1, BLK) if size % t == 0)


def rows_at(start, rows):
    return pl.ds(pl.multiple_of(start, rows), rows)


def whole(memory_space):
    return pl.BlockSpec(memory_space=memory_space)


def after(x, *earlier):
    return lax.optimization_barrier((x, *earlier))[0]


def slot_table(index_list, first_count, second_count):
    listing = index_list[0, 0]
    slots = listing.shape[0]
    flat = jnp.where(listing[:, 0] >= 0, listing[:, 0] * second_count + listing[:, 1], -1)
    positions = jnp.arange(first_count * second_count, dtype=jnp.int32)
    hits = flat[None, :] == positions[:, None]
    back_from = slots - jnp.arange(slots, dtype=jnp.int32)
    table = slots - jnp.sum(jnp.where(hits, back_from[None, :], 0), axis=1)
    count = jnp.sum((flat >= 0).astype(jnp.int32))
    return table, count.reshape(1)


def densify_kernel(mats, rows, cols, panels, *refs):
    tables, blocks = refs[:mats], refs[mats : 2 * mats]
    outs = refs[-4 - mats : -4]
    store, stage, in_sem, out_sem = refs[-4:]
    slots = blocks[0].shape[0]
    loads = [
        pltpu.make_async_copy(blocks[m], store.at[m, pl.ds(0, slots)], in_sem.at[m])
        for m in range(mats)
    ]
    for load in loads:
        load.start()
    high = rows // panels
    writes = []
    for m in range(mats):
        store[m, slots] = jnp.zeros((BLK, BLK), jnp.bfloat16)
        loads[m].wait()
        for g in range(panels):
            if m:
                writes[(m - 1) * panels + g].wait()

            def fill(r, carry, m=m, g=g):
                for j in range(cols):
                    slot = tables[m][(g * high + r) * cols + j]
                    stage[g, rows_at(r * BLK, BLK), j * BLK : (j + 1) * BLK] = store[m, slot]
                return carry

            lax.fori_loop(0, high, fill, 0)
            write = pltpu.make_async_copy(
                stage.at[g], outs[m].at[pl.ds(g * high * BLK, high * BLK)], out_sem.at[g]
            )
            write.start()
            writes.append(write)
    for write in writes[-panels:]:
        write.wait()


def densify(tables, blocks, rows, cols, *earlier):
    mats = len(blocks)
    slots = blocks[0].shape[0]
    panels = 4 if rows % 4 == 0 else 1
    shape = jax.ShapeDtypeStruct((rows * BLK, cols * BLK), jnp.bfloat16)
    return pl.pallas_call(
        functools.partial(densify_kernel, mats, rows, cols, panels),
        out_shape=(shape,) * mats,
        in_specs=[whole(SM)] * mats + [whole(pl.ANY)] * (mats + len(earlier)),
        out_specs=(whole(pl.ANY),) * mats,
        scratch_shapes=[
            VM((mats, slots + 1, BLK, BLK), jnp.bfloat16),
            VM((panels, rows // panels * BLK, cols * BLK), jnp.bfloat16),
            pltpu.SemaphoreType.DMA((mats,)),
            pltpu.SemaphoreType.DMA((panels,)),
        ],
        compiler_params=params(),
        cost_estimate=cost(0, mats * (slots + rows * cols) * BLK * BLK * 2),
    )(*tables, *blocks, *earlier)


def stream(copies, first):
    for copy in first:
        copy.start()
    copies[0].start()
    for copy in first:
        copy.wait()
    for n, copy in enumerate(copies):
        if n == 0:
            for ahead in copies[1:AHEAD]:
                ahead.start()
        copy.wait()
        if n + AHEAD < len(copies):
            copies[n + AHEAD].start()
        yield n


def product(panel, held, transposed):
    dims = (((1,), (1 if transposed else 0,)), ((), ()))
    return lax.dot_general(panel, held[...], dims, preferred_element_type=jnp.float32)


def project_kernel(transposed, tile, core_ref, panel, weight, *refs):
    mine_ref, other_ref = refs[-5:-3]
    held_panel, store, sem = refs[-3:]
    load = pltpu.make_async_copy(panel, held_panel, sem.at[0])
    is_first = core_ref[0] == 0
    half = panel.shape[0] // 2
    spans = [pl.ds(i * tile, tile) for i in range(mine_ref.shape[1] // tile)]
    places = [(at,) if transposed else (slice(None), at) for at in spans]
    copies = [
        pltpu.make_async_copy(weight.at[at], store.at[at], sem.at[1 + i])
        for i, at in enumerate(places)
    ]
    for i in stream(copies, [load]):
        full = product(held_panel[...], store.at[places[i]], transposed)
        first, second = full[:half], full[half:]
        mine_ref[:, spans[i]] = jnp.where(is_first, first, second)
        other_ref[:, spans[i]] = jnp.where(is_first, second, first).astype(jnp.bfloat16)


def project(core, panel, weight, transposed, *earlier):
    tokens, depth = panel.shape
    width = weight.shape[0] if transposed else weight.shape[1]
    tile = tile_of(width, PROJECT_TILE)
    shape = (tokens // 2, width)
    return pl.pallas_call(
        functools.partial(project_kernel, transposed, tile),
        out_shape=(
            jax.ShapeDtypeStruct(shape, jnp.float32),
            jax.ShapeDtypeStruct(shape, jnp.bfloat16),
        ),
        in_specs=[whole(SM)] + [whole(pl.ANY)] * (2 + len(earlier)),
        out_specs=(whole(VM),) * 2,
        scratch_shapes=[
            VM(panel.shape, jnp.bfloat16),
            VM(weight.shape, jnp.bfloat16),
            pltpu.SemaphoreType.DMA((1 + width // tile,)),
        ],
        compiler_params=params(),
        cost_estimate=cost(2 * tokens * depth * width, 2 * depth * width),
    )(core, panel, weight, *earlier)


def project_blocks_kernel(transposed, rows, cols, high, ring, core_ref, table, panel, blocks, *refs):
    mine_ref, other_ref, dense = refs[-8:-5]
    store, panel_ref, stage, in_sem, out_sem = refs[-5:]
    slots = blocks.shape[0]
    load = pltpu.make_async_copy(blocks, store.at[pl.ds(0, slots)], in_sem.at[0])
    load.start()
    load_panel = pltpu.make_async_copy(panel, panel_ref, in_sem.at[1])
    load_panel.start()
    store[slots] = jnp.zeros((BLK, BLK), jnp.bfloat16)
    is_first = core_ref[0] == 0
    half = panel_ref.shape[0] // 2
    load.wait()
    load_panel.wait()
    writes = []
    for i in range((rows if transposed else cols) // high):
        held = stage.at[i % ring]
        if i >= ring:
            writes[i - ring].wait()
        for far in range(cols if transposed else rows):
            for near in range(high):
                r, c = (i * high + near, far) if transposed else (far, i * high + near)
                r_at, c_at = (near, far) if transposed else (far, near)
                held[r_at * BLK : (r_at + 1) * BLK, c_at * BLK : (c_at + 1) * BLK] = store[
                    table[r * cols + c]
                ]
        at = pl.ds(i * high * BLK, high * BLK)
        write = pltpu.make_async_copy(
            held, dense.at[at] if transposed else dense.at[:, at], out_sem.at[i % ring]
        )
        write.start()
        writes.append(write)
        full = product(panel_ref[...], held, transposed)
        first, second = full[:half], full[half:]
        mine_ref[:, at] = jnp.where(is_first, first, second)
        other_ref[:, at] = jnp.where(is_first, second, first).astype(jnp.bfloat16)
    for write in writes[-ring:]:
        write.wait()


def project_blocks(core, panel, table, blocks, rows, cols, transposed, *earlier):
    tokens, _ = panel.shape
    slots = blocks.shape[0]
    cut, across = (rows, cols) if transposed else (cols, rows)
    high = tile_of(cut * BLK, 512) // BLK
    ring = min(3, cut // high)
    tile_shape = (high * BLK, across * BLK) if transposed else (across * BLK, high * BLK)
    shape = (tokens // 2, cut * BLK)
    return pl.pallas_call(
        functools.partial(project_blocks_kernel, transposed, rows, cols, high, ring),
        out_shape=(
            jax.ShapeDtypeStruct(shape, jnp.float32),
            jax.ShapeDtypeStruct(shape, jnp.bfloat16),
            jax.ShapeDtypeStruct((rows * BLK, cols * BLK), jnp.bfloat16),
        ),
        in_specs=[whole(SM)] * 2 + [whole(pl.ANY)] * (2 + len(earlier)),
        out_specs=(whole(VM), whole(VM), whole(pl.ANY)),
        scratch_shapes=[
            VM((slots + 1, BLK, BLK), jnp.bfloat16),
            VM(panel.shape, jnp.bfloat16),
            VM((ring, *tile_shape), jnp.bfloat16),
            pltpu.SemaphoreType.DMA((2,)),
            pltpu.SemaphoreType.DMA((ring,)),
        ],
        compiler_params=params(),
        cost_estimate=cost(2 * tokens * rows * cols * BLK * BLK, rows * cols * BLK * BLK * 4),
    )(core, table, panel, blocks, *earlier)


def back_kernel(transposed, n_pieces, mats, chunks, tile, core_ref, *refs):
    pieces, weights = refs[:n_pieces], refs[n_pieces : n_pieces + mats]
    outs = refs[-4 - chunks : -4]
    store, panel, sem, piece_sem = refs[-4:]
    half, depth = pieces[0].shape[1:]
    loads = [
        pltpu.make_async_copy(
            piece.at[w],
            panel.at[pl.ds(k * half, half), pl.ds(w * depth, depth)],
            piece_sem.at[w * n_pieces + k],
        )
        for w in range(mats)
        for k, piece in enumerate(pieces)
    ]
    is_first = core_ref[0] == 0
    rows = n_pieces * half // chunks
    copies = []
    for i in range(outs[0].shape[1] // tile):
        at = pl.ds(i * tile, tile)
        for w, weight in enumerate(weights):
            deep = pl.ds(w * depth, depth)
            source = weight.at[at] if transposed else weight.at[:, at]
            target = store.at[at, deep] if transposed else store.at[deep, at]
            copies.append(pltpu.make_async_copy(source, target, sem.at[w, i]))
    for n in stream(copies, loads):
        if n % mats < mats - 1:
            continue
        at = pl.ds(n // mats * tile, tile)
        total = product(panel[...], store.at[at] if transposed else store.at[:, at], transposed)
        mine, other = total[:half], total[half:]
        ordered = (jnp.where(is_first, mine, other), jnp.where(is_first, other, mine))
        for d in range(chunks):
            which, start = divmod(d * rows, half)
            outs[d][:, at] = ordered[which][start : start + rows].astype(outs[d].dtype)


def back(core, pieces, weights, chunks, transposed, *earlier):
    n_pieces, mats = len(pieces), len(weights)
    half, depth = pieces[0].shape[1:]
    width = weights[0].shape[0] if transposed else weights[0].shape[1]
    tile = tile_of(width, BACK_TILE)
    rows = n_pieces * half // chunks
    shapes = tuple(
        jax.ShapeDtypeStruct((rows, width), jnp.bfloat16 if d else jnp.float32)
        for d in range(chunks)
    )
    return pl.pallas_call(
        functools.partial(back_kernel, transposed, n_pieces, mats, chunks, tile),
        out_shape=shapes,
        in_specs=[whole(SM)] + [whole(pl.ANY)] * (n_pieces + mats + len(earlier)),
        out_specs=(whole(VM),) * chunks,
        scratch_shapes=[
            VM((width, mats * depth) if transposed else (mats * depth, width), jnp.bfloat16),
            VM((n_pieces * half, mats * depth), jnp.bfloat16),
            pltpu.SemaphoreType.DMA((mats, width // tile)),
            pltpu.SemaphoreType.DMA((mats * n_pieces,)),
        ],
        compiler_params=params(),
        cost_estimate=cost(
            2 * n_pieces * half * depth * width * mats, 2 * depth * width * mats
        ),
    )(core, *pieces, *weights, *earlier)


def pair_sum(mine, other, token=None):
    total = mine + other.astype(jnp.float32)
    if token is not None:
        total = total + token
    return total.astype(jnp.bfloat16)


def hold_kernel(*refs):
    del refs


def hold(x, *earlier):
    return pl.pallas_call(
        hold_kernel,
        out_shape=jax.ShapeDtypeStruct(x.shape, x.dtype),
        in_specs=[whole(pl.ANY)] * (1 + len(earlier)),
        out_specs=whole(pl.ANY),
        input_output_aliases={0: 0},
        compiler_params=params(),
        cost_estimate=pl.CostEstimate(flops=0, bytes_accessed=MARK, transcendentals=0),
    )(x, *earlier)


def sum_kernel(counts, *refs):
    at = 0
    for out, count in zip(refs[len(refs) - len(counts) :], counts):
        out[...] = add_up([ref[...] for ref in refs[at : at + count]]).astype(out.dtype)
        at += count


def sum_chunks(lists, *earlier):
    counts = [len(parts) for parts in lists]
    parts = [part for parts in lists for part in parts]
    return pl.pallas_call(
        functools.partial(sum_kernel, counts),
        out_shape=tuple(jax.ShapeDtypeStruct(p[0].shape, jnp.bfloat16) for p in lists),
        in_specs=[whole(VM)] * len(parts) + [whole(pl.ANY)] * len(earlier),
        out_specs=(whole(VM),) * len(lists),
        compiler_params=params(),
        cost_estimate=cost(0, parts[0].size * 10),
    )(*parts, *earlier)


def mark(*earlier):
    total = 0.0
    for x in earlier:
        corner = lax.slice(x, (0,) * x.ndim, (1,) * x.ndim).reshape(())
        total = total + jnp.abs(corner.astype(jnp.float32))
    return lax.optimization_barrier(jnp.minimum(total, 0.0))


def across(rows, width):
    return pl.BlockSpec((rows, tile_of(width, POINT_WIDE)), lambda i: (0, i))


def hidden_kernel(n_sum, *refs):
    gate = add_up([ref[...] for ref in refs[:n_sum]])
    up = add_up([ref[...] for ref in refs[n_sum : 2 * n_sum]])
    refs[-1][0] = (gate * jax.nn.sigmoid(gate) * up).astype(jnp.bfloat16)


def slopes_kernel(n_sum, *refs):
    gate = add_up([ref[...] for ref in refs[:n_sum]])
    up = add_up([ref[...] for ref in refs[n_sum : 2 * n_sum]])
    sigma = jax.nn.sigmoid(gate)
    refs[-2][...] = up * sigma * (1.0 + gate * (1.0 - sigma))
    refs[-1][...] = gate * sigma


def pointwise(kernel, gates, ups, outs, *earlier):
    rows, width = gates[0].shape
    return pl.pallas_call(
        functools.partial(kernel, len(gates)),
        out_shape=tuple(shape for shape, _ in outs),
        grid=(width // tile_of(width, POINT_WIDE),),
        in_specs=[across(rows, width)] * (2 * len(gates)) + [whole(pl.ANY)] * len(earlier),
        out_specs=tuple(spec for _, spec in outs),
        compiler_params=params(),
        cost_estimate=cost(0, rows * width * 30),
    )(*gates, *ups, *earlier)


def act(gates, ups, *earlier):
    rows, width = gates[0].shape
    spec = pl.BlockSpec((1, rows, tile_of(width, POINT_WIDE)), lambda i: (0, 0, i))
    outs = [(jax.ShapeDtypeStruct((1, rows, width), jnp.bfloat16), spec)]
    return pointwise(hidden_kernel, gates, ups, outs, *earlier)[0]


def slopes(gates, ups, *earlier):
    rows, width = gates[0].shape
    out = (jax.ShapeDtypeStruct((rows, width), jnp.float32), across(rows, width))
    return pointwise(slopes_kernel, gates, ups, [out, out], *earlier)


def grads_kernel(n_sum, *refs):
    sums, (by_gate_ref, by_up_ref) = refs[:n_sum], refs[n_sum : n_sum + 2]
    both_ref = refs[-1]
    span = slice(None)
    grad_hidden = add_up([ref[:, span] for ref in sums])
    both_ref[0, :, span] = (grad_hidden * by_gate_ref[:, span]).astype(jnp.bfloat16)
    both_ref[1, :, span] = (grad_hidden * by_up_ref[:, span]).astype(jnp.bfloat16)


def act_grads(sums, by_gate, by_up, *earlier):
    return pl.pallas_call(
        functools.partial(grads_kernel, len(sums)),
        out_shape=jax.ShapeDtypeStruct((2, *by_gate.shape), jnp.bfloat16),
        grid=(by_gate.shape[1] // tile_of(by_gate.shape[1], POINT_WIDE),),
        in_specs=[across(*by_gate.shape)] * (len(sums) + 2) + [whole(pl.ANY)] * len(earlier),
        out_specs=pl.BlockSpec(
            (2, by_gate.shape[0], tile_of(by_gate.shape[1], POINT_WIDE)), lambda i: (0, 0, i)
        ),
        compiler_params=params(),
        cost_estimate=cost(0, by_gate.size * 20),
    )(*sums, by_gate, by_up, *earlier)


def own_order(core, ref):
    half = ref.shape[0] // 2
    return [ref.at[rows_at(core * half, half)], ref.at[rows_at((1 - core) * half, half)]]


def block_grad_kernel(mats, n_left, n_right, scale, cols, wide, core_ref, *refs):
    tables, counts = refs[:mats], refs[mats : 2 * mats]
    lefts = refs[2 * mats : 2 * mats + n_left]
    rights = refs[2 * mats + n_left : 2 * mats + n_left + n_right]
    outs, stores = refs[-6 - 2 * mats : -6 - mats], refs[-6 - mats : -6]
    left, right, turned, in_sem, left_sem, out_sem = refs[-6:]
    core = core_ref[0]
    slots = outs[0].shape[0]
    length, width = left.shape[1], right.shape[2]
    tall = tile_of(length, 512)

    def rows_of(refs, m):
        rows = []
        for ref in refs:
            rows += own_order(core, ref) if len(ref.shape) == 2 else [ref.at[m]]
        return rows

    def loads(sources, target, sem):
        rows = sources[0].shape[0]
        copies = [
            pltpu.make_async_copy(source, target.at[pl.ds(k * rows, rows)], sem.at[k])
            for k, source in enumerate(sources)
        ]
        return copies

    left_loads = loads(rows_of(lefts, 0), left, left_sem)
    right_loads = [loads(rows_of(rights, m), right.at[m], in_sem.at[m]) for m in range(mats)]
    for load in left_loads + right_loads[0]:
        load.start()

    def clear(slot, carry, m):
        stores[m][slot] = jnp.zeros((BLK, BLK), jnp.bfloat16)
        return carry

    for m in range(mats):
        lax.fori_loop(counts[m][0], slots, functools.partial(clear, m=m), 0)
    for load in left_loads:
        load.wait()
    for a in range(length // tall):
        span = slice(a * tall, (a + 1) * tall)
        turned[span, :] = left[:, span].T

    copies = []
    for m in range(mats):
        for load in right_loads[m]:
            load.wait()
        if m + 1 < mats:
            for load in right_loads[m + 1]:
                load.start()

        def column(at, carry, m=m):
            span = pl.ds(pl.multiple_of(at * wide, wide), wide)
            for a in range(length // tall):
                full = jnp.dot(
                    turned[a * tall : (a + 1) * tall, :],
                    right[m, :, span],
                    preferred_element_type=jnp.float32,
                )
                full = (full * scale).astype(jnp.bfloat16)
                for di in range(tall // BLK):
                    for dj in range(wide // BLK):
                        row = a * (tall // BLK) + di
                        slot = tables[m][row * cols + at * (wide // BLK) + dj]
                        stores[m][slot] = full[
                            di * BLK : (di + 1) * BLK, dj * BLK : (dj + 1) * BLK
                        ]
            return carry

        lax.fori_loop(0, width // wide, column, 0)
        copies.append(
            pltpu.make_async_copy(stores[m].at[pl.ds(0, slots)], outs[m], out_sem.at[m])
        )
        copies[m].start()
    for copy in copies:
        copy.wait()


def block_grads(core, tables, counts, lefts, rights, slots, scale, *earlier):
    mats = len(tables)
    tokens = sum(a.shape[-2] for a in lefts)
    length, width = lefts[0].shape[-1], rights[0].shape[-1]
    wide = tile_of(width, GRAD_WIDE)
    n_rows = [sum(2 if a.ndim == 2 else 1 for a in side) for side in (lefts, rights)]
    return pl.pallas_call(
        functools.partial(
            block_grad_kernel,
            mats,
            len(lefts),
            len(rights),
            scale,
            width // BLK,
            wide,
        ),
        out_shape=(jax.ShapeDtypeStruct((slots, BLK, BLK), jnp.bfloat16),) * mats,
        in_specs=[whole(SM)] * (1 + 2 * mats)
        + [whole(pl.ANY)] * (len(lefts) + len(rights) + len(earlier)),
        out_specs=(whole(pl.ANY),) * mats,
        scratch_shapes=[VM((slots + 1, BLK, BLK), jnp.bfloat16)] * mats
        + [
            VM((tokens, length), jnp.bfloat16),
            VM((mats, tokens, width), jnp.bfloat16),
            VM((length, tokens), jnp.bfloat16),
            pltpu.SemaphoreType.DMA((mats, n_rows[1])),
            pltpu.SemaphoreType.DMA((n_rows[0],)),
            pltpu.SemaphoreType.DMA((mats,)),
        ],
        compiler_params=params(),
        cost_estimate=cost(2 * tokens * length * width * mats, slots * BLK * BLK * 2 * mats),
    )(core, *tables, *counts, *lefts, *rights, *earlier)


def shift(x, axis, by):
    n = lax.axis_size(axis)
    return lax.ppermute(x, axis, [(i, (i + by) % n) for i in range(n)])


def swap_cores(x):
    n = lax.axis_size("row")
    return lax.ppermute(x, "row", [(i, i ^ 1) for i in range(n)])


def add_up(parts):
    total = parts[0].astype(jnp.float32)
    for part in parts[1:]:
        total = total + part.astype(jnp.float32)
    return total


def z_order(n):
    return sorted(range(1, n), key=lambda d: (min(d, n - d), d))


def other_chips(sent):
    n = lax.axis_size("row")
    return [shift(sent, "row", 2 * s) for s in range(1, n // 2)]


def other_groups(x):
    return [shift(x, "dp", s) for s in range(1, lax.axis_size("dp"))]


def on_device(
    tokens, cotangent, gate_blocks, gate_index, up_blocks, up_index, down_blocks, down_index
):
    n_col = lax.axis_size("col")
    parts = 1
    chunks = n_col // parts
    core = lax.rem(lax.axis_index("row"), 2).astype(jnp.int32).reshape(1)
    feats = tokens.shape[1] // BLK
    units = FF // BLK // n_col
    width = units * BLK
    slots = gate_blocks.shape[2]
    group_rows = tokens.shape[0] * n_col
    scale = 1.0 / math.sqrt(group_rows * lax.axis_size("dp"))

    def gather(x):
        got = {0: x}
        for d in z_order(n_col):
            got[d] = shift(x, "col", d)
        return [
            jnp.concatenate([got[d] for d in range(p * chunks, (p + 1) * chunks)], axis=0)
            for p in range(parts)
        ]

    def scatter(cut):
        return [cut[0]] + [shift(cut[d], "col", -d) for d in z_order(n_col)]

    def far_pieces(pairs):
        pieces = []
        for s in range(lax.axis_size("dp") - 1):
            for far in pairs:
                pieces += [far[s], swap_cores(far[s])]
        return pieces

    gate_table, gate_count = slot_table(gate_index, feats, units)
    up_table, up_count = slot_table(up_index, feats, units)
    down_table, down_count = slot_table(down_index, units, feats)

    x_parts = gather(tokens)
    x_whole = jnp.concatenate(x_parts, axis=0)
    (w_gate,) = densify((gate_table,), (gate_blocks[0, 0],), feats, units)
    gate_mine, gate_other = project(core, x_whole, w_gate, False)
    gate_swapped = swap_cores(gate_other)
    gate_sent = pair_sum(gate_mine, gate_swapped)

    gate_got = other_chips(gate_sent)
    c_parts = gather(after(cotangent, x_whole))
    c_whole = jnp.concatenate(c_parts, axis=0)
    x_groups = [x_whole] + other_groups(x_whole)
    up_mine, up_other, w_up = project_blocks(
        core, x_whole, up_table, up_blocks[0, 0], feats, units, False, gate_sent
    )
    token = mark(*gate_got, c_whole, *x_groups[1:])
    up_swapped = swap_cores(up_other)
    up_sent = pair_sum(up_mine, up_swapped, token)

    up_got = other_chips(up_sent)
    c_groups = [c_whole] + other_groups(c_whole)
    back_mine, back_other, w_down = project_blocks(
        core, c_whole, down_table, down_blocks[0, 0], units, feats, True, up_sent
    )
    token = mark(*up_got, *c_groups[1:])
    back_swapped = swap_cores(back_other)
    back_sent = pair_sum(back_mine, back_swapped, token)

    back_got = other_chips(back_sent)
    gate_sums = [gate_mine, gate_swapped] + gate_got
    up_sums = [up_mine, up_swapped] + up_got
    hidden = act(gate_sums, up_sums, back_sent)
    hidden_far = other_groups(hidden)
    hidden_pieces = [hidden, swap_cores(hidden)]
    out_cut = back(core, hidden_pieces, [w_down], n_col, False)
    by_gate, by_up = slopes(gate_sums, up_sums, out_cut[0])
    grads = act_grads([back_mine, back_swapped] + back_got, by_gate, by_up)
    hidden_pieces += far_pieces([[hold(far, grads) for far in hidden_far]])

    grads_far = other_groups(grads)
    grad_pieces = [grads, swap_cores(grads)]
    (down_grad,) = block_grads(
        core,
        (down_table,),
        (down_count,),
        hidden_pieces,
        c_groups,
        slots,
        scale,
        grads,
    )
    in_cut = back(core, grad_pieces, [w_gate, w_up], n_col, True, down_grad)
    out_kept = scatter(out_cut)
    (output,) = sum_chunks([out_kept], in_cut[0])
    grads_far = [hold(far, output) for far in grads_far]
    gate_grad, up_grad = block_grads(
        core,
        (gate_table, up_table),
        (gate_count, up_count),
        x_groups,
        grad_pieces + far_pieces([grads_far]),
        slots,
        scale,
    )
    (input_grad,) = sum_chunks([scatter(in_cut)], gate_grad)
    shape = gate_blocks.shape
    return (
        output,
        input_grad,
        gate_grad.reshape(shape),
        up_grad.reshape(shape),
        down_grad.reshape(shape),
    )


def solution(mesh):
    return jax.shard_map(
        on_device,
        mesh=mesh,
        in_specs=(
            P(("dp", "col"), "row"),
            P(("dp", "col"), "row"),
            P("row", "col", None, None, None),
            P("row", "col", None, None),
            P("row", "col", None, None, None),
            P("row", "col", None, None),
            P("row", "col", None, None, None),
            P("row", "col", None, None),
        ),
        out_specs=(
            P(("dp", "col"), "row"),
            P(("dp", "col"), "row"),
            P("row", "col", None, None, None),
            P("row", "col", None, None, None),
            P("row", "col", None, None, None),
        ),
        check_vma=False,
    )
```

```python
import functools
import math

import jax
import jax.numpy as jnp
from jax import lax
from jax.experimental import pallas as pl
from jax.experimental.pallas import tpu as pltpu
from jax.sharding import PartitionSpec as P

BLK = 128
AHEAD = 3
PROJECT_TILE = 512
BACK_TILE = 512
GRAD_WIDE = 512
POINT_WIDE = 1792
COST = 0.000001
MARK = 200000
FF = 14336
VMEM_LIMIT = 56 * 1024 * 1024
VM = pltpu.VMEM
SM = pltpu.SMEM


def params():
    return pltpu.CompilerParams(vmem_limit_bytes=VMEM_LIMIT)


def cost(flops, nbytes):
    return pl.CostEstimate(
        flops=int(flops * COST), bytes_accessed=int(nbytes * COST), transcendentals=0
    )


def tile_of(size, largest):
    return max(t for t in range(BLK, largest + 1, BLK) if size % t == 0)


def rows_at(start, rows):
    return pl.ds(pl.multiple_of(start, rows), rows)


def whole(memory_space):
    return pl.BlockSpec(memory_space=memory_space)


def after(x, *earlier):
    return lax.optimization_barrier((x, *earlier))[0]


def slot_table(index_list, first_count, second_count):
    listing = index_list[0, 0]
    slots = listing.shape[0]
    flat = jnp.where(listing[:, 0] >= 0, listing[:, 0] * second_count + listing[:, 1], -1)
    positions = jnp.arange(first_count * second_count, dtype=jnp.int32)
    hits = flat[None, :] == positions[:, None]
    back_from = slots - jnp.arange(slots, dtype=jnp.int32)
    table = slots - jnp.sum(jnp.where(hits, back_from[None, :], 0), axis=1)
    count = jnp.sum((flat >= 0).astype(jnp.int32))
    return table, count.reshape(1)


def densify_kernel(mats, rows, cols, panels, *refs):
    tables, blocks = refs[:mats], refs[mats : 2 * mats]
    outs = refs[-4 - mats : -4]
    store, stage, in_sem, out_sem = refs[-4:]
    slots = blocks[0].shape[0]
    loads = [
        pltpu.make_async_copy(blocks[m], store.at[m, pl.ds(0, slots)], in_sem.at[m])
        for m in range(mats)
    ]
    for load in loads:
        load.start()
    high = rows // panels
    writes = []
    for m in range(mats):
        store[m, slots] = jnp.zeros((BLK, BLK), jnp.bfloat16)
        loads[m].wait()
        for g in range(panels):
            if m:
                writes[(m - 1) * panels + g].wait()

            def fill(r, carry, m=m, g=g):
                for j in range(cols):
                    slot = tables[m][(g * high + r) * cols + j]
                    stage[g, rows_at(r * BLK, BLK), j * BLK : (j + 1) * BLK] = store[m, slot]
                return carry

            lax.fori_loop(0, high, fill, 0)
            write = pltpu.make_async_copy(
                stage.at[g], outs[m].at[pl.ds(g * high * BLK, high * BLK)], out_sem.at[g]
            )
            write.start()
            writes.append(write)
    for write in writes[-panels:]:
        write.wait()


def densify(tables, blocks, rows, cols, *earlier):
    mats = len(blocks)
    slots = blocks[0].shape[0]
    panels = 4 if rows % 4 == 0 else 1
    shape = jax.ShapeDtypeStruct((rows * BLK, cols * BLK), jnp.bfloat16)
    return pl.pallas_call(
        functools.partial(densify_kernel, mats, rows, cols, panels),
        out_shape=(shape,) * mats,
        in_specs=[whole(SM)] * mats + [whole(pl.ANY)] * (mats + len(earlier)),
        out_specs=(whole(pl.ANY),) * mats,
        scratch_shapes=[
            VM((mats, slots + 1, BLK, BLK), jnp.bfloat16),
            VM((panels, rows // panels * BLK, cols * BLK), jnp.bfloat16),
            pltpu.SemaphoreType.DMA((mats,)),
            pltpu.SemaphoreType.DMA((panels,)),
        ],
        compiler_params=params(),
        cost_estimate=cost(0, mats * (slots + rows * cols) * BLK * BLK * 2),
    )(*tables, *blocks, *earlier)


def stream(copies, first):
    for copy in first:
        copy.start()
    copies[0].start()
    for copy in first:
        copy.wait()
    for n, copy in enumerate(copies):
        if n == 0:
            for ahead in copies[1:AHEAD]:
                ahead.start()
        copy.wait()
        if n + AHEAD < len(copies):
            copies[n + AHEAD].start()
        yield n


def product(panel, held, transposed):
    dims = (((1,), (1 if transposed else 0,)), ((), ()))
    return lax.dot_general(panel, held[...], dims, preferred_element_type=jnp.float32)


def project_kernel(transposed, tile, core_ref, panel, weight, *refs):
    mine_ref, other_ref = refs[-5:-3]
    held_panel, store, sem = refs[-3:]
    load = pltpu.make_async_copy(panel, held_panel, sem.at[0])
    is_first = core_ref[0] == 0
    half = panel.shape[0] // 2
    spans = [pl.ds(i * tile, tile) for i in range(mine_ref.shape[1] // tile)]
    places = [(at,) if transposed else (slice(None), at) for at in spans]
    copies = [
        pltpu.make_async_copy(weight.at[at], store.at[at], sem.at[1 + i])
        for i, at in enumerate(places)
    ]
    for i in stream(copies, [load]):
        full = product(held_panel[...], store.at[places[i]], transposed)
        first, second = full[:half], full[half:]
        mine_ref[:, spans[i]] = jnp.where(is_first, first, second)
        other_ref[:, spans[i]] = jnp.where(is_first, second, first).astype(jnp.bfloat16)


def project(core, panel, weight, transposed, *earlier):
    tokens, depth = panel.shape
    width = weight.shape[0] if transposed else weight.shape[1]
    tile = tile_of(width, PROJECT_TILE)
    shape = (tokens // 2, width)
    return pl.pallas_call(
        functools.partial(project_kernel, transposed, tile),
        out_shape=(
            jax.ShapeDtypeStruct(shape, jnp.float32),
            jax.ShapeDtypeStruct(shape, jnp.bfloat16),
        ),
        in_specs=[whole(SM)] + [whole(pl.ANY)] * (2 + len(earlier)),
        out_specs=(whole(VM),) * 2,
        scratch_shapes=[
            VM(panel.shape, jnp.bfloat16),
            VM(weight.shape, jnp.bfloat16),
            pltpu.SemaphoreType.DMA((1 + width // tile,)),
        ],
        compiler_params=params(),
        cost_estimate=cost(2 * tokens * depth * width, 2 * depth * width),
    )(core, panel, weight, *earlier)


def project_blocks_kernel(transposed, rows, cols, high, ring, core_ref, table, panel, blocks, *refs):
    mine_ref, other_ref, dense = refs[-8:-5]
    store, panel_ref, stage, in_sem, out_sem = refs[-5:]
    slots = blocks.shape[0]
    load = pltpu.make_async_copy(blocks, store.at[pl.ds(0, slots)], in_sem.at[0])
    load.start()
    load_panel = pltpu.make_async_copy(panel, panel_ref, in_sem.at[1])
    load_panel.start()
    store[slots] = jnp.zeros((BLK, BLK), jnp.bfloat16)
    is_first = core_ref[0] == 0
    half = panel_ref.shape[0] // 2
    load.wait()
    load_panel.wait()
    writes = []
    for i in range((rows if transposed else cols) // high):
        held = stage.at[i % ring]
        if i >= ring:
            writes[i - ring].wait()
        for far in range(cols if transposed else rows):
            for near in range(high):
                r, c = (i * high + near, far) if transposed else (far, i * high + near)
                r_at, c_at = (near, far) if transposed else (far, near)
                held[r_at * BLK : (r_at + 1) * BLK, c_at * BLK : (c_at + 1) * BLK] = store[
                    table[r * cols + c]
                ]
        at = pl.ds(i * high * BLK, high * BLK)
        write = pltpu.make_async_copy(
            held, dense.at[at] if transposed else dense.at[:, at], out_sem.at[i % ring]
        )
        write.start()
        writes.append(write)
        full = product(panel_ref[...], held, transposed)
        first, second = full[:half], full[half:]
        mine_ref[:, at] = jnp.where(is_first, first, second)
        other_ref[:, at] = jnp.where(is_first, second, first).astype(jnp.bfloat16)
    for write in writes[-ring:]:
        write.wait()


def project_blocks(core, panel, table, blocks, rows, cols, transposed, *earlier):
    tokens, _ = panel.shape
    slots = blocks.shape[0]
    cut, across = (rows, cols) if transposed else (cols, rows)
    high = tile_of(cut * BLK, 512) // BLK
    ring = min(3, cut // high)
    tile_shape = (high * BLK, across * BLK) if transposed else (across * BLK, high * BLK)
    shape = (tokens // 2, cut * BLK)
    return pl.pallas_call(
        functools.partial(project_blocks_kernel, transposed, rows, cols, high, ring),
        out_shape=(
            jax.ShapeDtypeStruct(shape, jnp.float32),
            jax.ShapeDtypeStruct(shape, jnp.bfloat16),
            jax.ShapeDtypeStruct((rows * BLK, cols * BLK), jnp.bfloat16),
        ),
        in_specs=[whole(SM)] * 2 + [whole(pl.ANY)] * (2 + len(earlier)),
        out_specs=(whole(VM), whole(VM), whole(pl.ANY)),
        scratch_shapes=[
            VM((slots + 1, BLK, BLK), jnp.bfloat16),
            VM(panel.shape, jnp.bfloat16),
            VM((ring, *tile_shape), jnp.bfloat16),
            pltpu.SemaphoreType.DMA((2,)),
            pltpu.SemaphoreType.DMA((ring,)),
        ],
        compiler_params=params(),
        cost_estimate=cost(2 * tokens * rows * cols * BLK * BLK, rows * cols * BLK * BLK * 4),
    )(core, table, panel, blocks, *earlier)


def back_kernel(transposed, n_pieces, mats, chunks, tile, core_ref, *refs):
    pieces, weights = refs[:n_pieces], refs[n_pieces : n_pieces + mats]
    outs = refs[-4 - chunks : -4]
    store, panel, sem, piece_sem = refs[-4:]
    half, depth = pieces[0].shape[1:]
    loads = [
        pltpu.make_async_copy(
            piece.at[w],
            panel.at[pl.ds(k * half, half), pl.ds(w * depth, depth)],
            piece_sem.at[w * n_pieces + k],
        )
        for w in range(mats)
        for k, piece in enumerate(pieces)
    ]
    is_first = core_ref[0] == 0
    rows = n_pieces * half // chunks
    copies = []
    for i in range(outs[0].shape[1] // tile):
        at = pl.ds(i * tile, tile)
        for w, weight in enumerate(weights):
            deep = pl.ds(w * depth, depth)
            source = weight.at[at] if transposed else weight.at[:, at]
            target = store.at[at, deep] if transposed else store.at[deep, at]
            copies.append(pltpu.make_async_copy(source, target, sem.at[w, i]))
    for n in stream(copies, loads):
        if n % mats < mats - 1:
            continue
        at = pl.ds(n // mats * tile, tile)
        total = product(panel[...], store.at[at] if transposed else store.at[:, at], transposed)
        mine, other = total[:half], total[half:]
        ordered = (jnp.where(is_first, mine, other), jnp.where(is_first, other, mine))
        for d in range(chunks):
            which, start = divmod(d * rows, half)
            outs[d][:, at] = ordered[which][start : start + rows].astype(outs[d].dtype)


def back(core, pieces, weights, chunks, transposed, *earlier):
    n_pieces, mats = len(pieces), len(weights)
    half, depth = pieces[0].shape[1:]
    width = weights[0].shape[0] if transposed else weights[0].shape[1]
    tile = tile_of(width, BACK_TILE)
    rows = n_pieces * half // chunks
    shapes = tuple(
        jax.ShapeDtypeStruct((rows, width), jnp.bfloat16 if d else jnp.float32)
        for d in range(chunks)
    )
    return pl.pallas_call(
        functools.partial(back_kernel, transposed, n_pieces, mats, chunks, tile),
        out_shape=shapes,
        in_specs=[whole(SM)] + [whole(pl.ANY)] * (n_pieces + mats + len(earlier)),
        out_specs=(whole(VM),) * chunks,
        scratch_shapes=[
            VM((width, mats * depth) if transposed else (mats * depth, width), jnp.bfloat16),
            VM((n_pieces * half, mats * depth), jnp.bfloat16),
            pltpu.SemaphoreType.DMA((mats, width // tile)),
            pltpu.SemaphoreType.DMA((mats * n_pieces,)),
        ],
        compiler_params=params(),
        cost_estimate=cost(
            2 * n_pieces * half * depth * width * mats, 2 * depth * width * mats
        ),
    )(core, *pieces, *weights, *earlier)


def pair_sum(mine, other, token=None):
    total = mine + other.astype(jnp.float32)
    if token is not None:
        total = total + token
    return total.astype(jnp.bfloat16)


def hold_kernel(*refs):
    del refs


def hold(x, *earlier):
    return pl.pallas_call(
        hold_kernel,
        out_shape=jax.ShapeDtypeStruct(x.shape, x.dtype),
        in_specs=[whole(pl.ANY)] * (1 + len(earlier)),
        out_specs=whole(pl.ANY),
        input_output_aliases={0: 0},
        compiler_params=params(),
        cost_estimate=pl.CostEstimate(flops=0, bytes_accessed=MARK, transcendentals=0),
    )(x, *earlier)


def sum_kernel(counts, *refs):
    at = 0
    for out, count in zip(refs[len(refs) - len(counts) :], counts):
        out[...] = add_up([ref[...] for ref in refs[at : at + count]]).astype(out.dtype)
        at += count


def sum_chunks(lists, *earlier):
    counts = [len(parts) for parts in lists]
    parts = [part for parts in lists for part in parts]
    return pl.pallas_call(
        functools.partial(sum_kernel, counts),
        out_shape=tuple(jax.ShapeDtypeStruct(p[0].shape, jnp.bfloat16) for p in lists),
        in_specs=[whole(VM)] * len(parts) + [whole(pl.ANY)] * len(earlier),
        out_specs=(whole(VM),) * len(lists),
        compiler_params=params(),
        cost_estimate=cost(0, parts[0].size * 10),
    )(*parts, *earlier)


def mark(*earlier):
    total = 0.0
    for x in earlier:
        corner = x[(0,) * (x.ndim - 2)][:16, :BLK]
        total = total + jnp.sum(jnp.abs(corner.astype(jnp.float32)))
    return lax.optimization_barrier(jnp.minimum(total, 0.0))


def across(rows, width):
    return pl.BlockSpec((rows, tile_of(width, POINT_WIDE)), lambda i: (0, i))


def hidden_kernel(n_sum, *refs):
    gate = add_up([ref[...] for ref in refs[:n_sum]])
    up = add_up([ref[...] for ref in refs[n_sum : 2 * n_sum]])
    refs[-1][0] = (gate * jax.nn.sigmoid(gate) * up).astype(jnp.bfloat16)


def slopes_kernel(n_sum, *refs):
    gate = add_up([ref[...] for ref in refs[:n_sum]])
    up = add_up([ref[...] for ref in refs[n_sum : 2 * n_sum]])
    sigma = jax.nn.sigmoid(gate)
    refs[-2][...] = up * sigma * (1.0 + gate * (1.0 - sigma))
    refs[-1][...] = gate * sigma


def pointwise(kernel, gates, ups, outs, *earlier):
    rows, width = gates[0].shape
    return pl.pallas_call(
        functools.partial(kernel, len(gates)),
        out_shape=tuple(shape for shape, _ in outs),
        grid=(width // tile_of(width, POINT_WIDE),),
        in_specs=[across(rows, width)] * (2 * len(gates)) + [whole(pl.ANY)] * len(earlier),
        out_specs=tuple(spec for _, spec in outs),
        compiler_params=params(),
        cost_estimate=cost(0, rows * width * 30),
    )(*gates, *ups, *earlier)


def act(gates, ups, *earlier):
    rows, width = gates[0].shape
    spec = pl.BlockSpec((1, rows, tile_of(width, POINT_WIDE)), lambda i: (0, 0, i))
    outs = [(jax.ShapeDtypeStruct((1, rows, width), jnp.bfloat16), spec)]
    return pointwise(hidden_kernel, gates, ups, outs, *earlier)[0]


def slopes(gates, ups, *earlier):
    rows, width = gates[0].shape
    out = (jax.ShapeDtypeStruct((rows, width), jnp.float32), across(rows, width))
    return pointwise(slopes_kernel, gates, ups, [out, out], *earlier)


def grads_kernel(n_sum, *refs):
    sums, (by_gate_ref, by_up_ref) = refs[:n_sum], refs[n_sum : n_sum + 2]
    both_ref = refs[-1]
    span = slice(None)
    grad_hidden = add_up([ref[:, span] for ref in sums])
    both_ref[0, :, span] = (grad_hidden * by_gate_ref[:, span]).astype(jnp.bfloat16)
    both_ref[1, :, span] = (grad_hidden * by_up_ref[:, span]).astype(jnp.bfloat16)


def act_grads(sums, by_gate, by_up, *earlier):
    return pl.pallas_call(
        functools.partial(grads_kernel, len(sums)),
        out_shape=jax.ShapeDtypeStruct((2, *by_gate.shape), jnp.bfloat16),
        grid=(by_gate.shape[1] // tile_of(by_gate.shape[1], POINT_WIDE),),
        in_specs=[across(*by_gate.shape)] * (len(sums) + 2) + [whole(pl.ANY)] * len(earlier),
        out_specs=pl.BlockSpec(
            (2, by_gate.shape[0], tile_of(by_gate.shape[1], POINT_WIDE)), lambda i: (0, 0, i)
        ),
        compiler_params=params(),
        cost_estimate=cost(0, by_gate.size * 20),
    )(*sums, by_gate, by_up, *earlier)


def own_order(core, ref):
    half = ref.shape[0] // 2
    return [ref.at[rows_at(core * half, half)], ref.at[rows_at((1 - core) * half, half)]]


def block_grad_kernel(mats, n_left, n_right, scale, cols, wide, core_ref, *refs):
    tables, counts = refs[:mats], refs[mats : 2 * mats]
    lefts = refs[2 * mats : 2 * mats + n_left]
    rights = refs[2 * mats + n_left : 2 * mats + n_left + n_right]
    outs, stores = refs[-6 - 2 * mats : -6 - mats], refs[-6 - mats : -6]
    left, right, turned, in_sem, left_sem, out_sem = refs[-6:]
    core = core_ref[0]
    slots = outs[0].shape[0]
    length, width = left.shape[1], right.shape[2]
    tall = tile_of(length, 512)

    def rows_of(refs, m):
        rows = []
        for ref in refs:
            rows += own_order(core, ref) if len(ref.shape) == 2 else [ref.at[m]]
        return rows

    def loads(sources, target, sem):
        rows = sources[0].shape[0]
        copies = [
            pltpu.make_async_copy(source, target.at[pl.ds(k * rows, rows)], sem.at[k])
            for k, source in enumerate(sources)
        ]
        return copies

    left_loads = loads(rows_of(lefts, 0), left, left_sem)
    right_loads = [loads(rows_of(rights, m), right.at[m], in_sem.at[m]) for m in range(mats)]
    for load in left_loads + right_loads[0]:
        load.start()

    def clear(slot, carry, m):
        stores[m][slot] = jnp.zeros((BLK, BLK), jnp.bfloat16)
        return carry

    for m in range(mats):
        lax.fori_loop(counts[m][0], slots, functools.partial(clear, m=m), 0)
    for load in left_loads:
        load.wait()
    for a in range(length // tall):
        span = slice(a * tall, (a + 1) * tall)
        turned[span, :] = left[:, span].T

    copies = []
    for m in range(mats):
        for load in right_loads[m]:
            load.wait()
        if m + 1 < mats:
            for load in right_loads[m + 1]:
                load.start()

        def column(at, carry, m=m):
            span = pl.ds(pl.multiple_of(at * wide, wide), wide)
            for a in range(length // tall):
                full = jnp.dot(
                    turned[a * tall : (a + 1) * tall, :],
                    right[m, :, span],
                    preferred_element_type=jnp.float32,
                )
                full = (full * scale).astype(jnp.bfloat16)
                for di in range(tall // BLK):
                    for dj in range(wide // BLK):
                        row = a * (tall // BLK) + di
                        slot = tables[m][row * cols + at * (wide // BLK) + dj]
                        stores[m][slot] = full[
                            di * BLK : (di + 1) * BLK, dj * BLK : (dj + 1) * BLK
                        ]
            return carry

        lax.fori_loop(0, width // wide, column, 0)
        copies.append(
            pltpu.make_async_copy(stores[m].at[pl.ds(0, slots)], outs[m], out_sem.at[m])
        )
        copies[m].start()
    for copy in copies:
        copy.wait()


def block_grads(core, tables, counts, lefts, rights, slots, scale, *earlier):
    mats = len(tables)
    tokens = sum(a.shape[-2] for a in lefts)
    length, width = lefts[0].shape[-1], rights[0].shape[-1]
    wide = tile_of(width, GRAD_WIDE)
    n_rows = [sum(2 if a.ndim == 2 else 1 for a in side) for side in (lefts, rights)]
    return pl.pallas_call(
        functools.partial(
            block_grad_kernel,
            mats,
            len(lefts),
            len(rights),
            scale,
            width // BLK,
            wide,
        ),
        out_shape=(jax.ShapeDtypeStruct((slots, BLK, BLK), jnp.bfloat16),) * mats,
        in_specs=[whole(SM)] * (1 + 2 * mats)
        + [whole(pl.ANY)] * (len(lefts) + len(rights) + len(earlier)),
        out_specs=(whole(pl.ANY),) * mats,
        scratch_shapes=[VM((slots + 1, BLK, BLK), jnp.bfloat16)] * mats
        + [
            VM((tokens, length), jnp.bfloat16),
            VM((mats, tokens, width), jnp.bfloat16),
            VM((length, tokens), jnp.bfloat16),
            pltpu.SemaphoreType.DMA((mats, n_rows[1])),
            pltpu.SemaphoreType.DMA((n_rows[0],)),
            pltpu.SemaphoreType.DMA((mats,)),
        ],
        compiler_params=params(),
        cost_estimate=cost(2 * tokens * length * width * mats, slots * BLK * BLK * 2 * mats),
    )(core, *tables, *counts, *lefts, *rights, *earlier)


def shift(x, axis, by):
    n = lax.axis_size(axis)
    return lax.ppermute(x, axis, [(i, (i + by) % n) for i in range(n)])


def swap_cores(x):
    n = lax.axis_size("row")
    return lax.ppermute(x, "row", [(i, i ^ 1) for i in range(n)])


def add_up(parts):
    total = parts[0].astype(jnp.float32)
    for part in parts[1:]:
        total = total + part.astype(jnp.float32)
    return total


def z_order(n):
    return sorted(range(1, n), key=lambda d: (min(d, n - d), d))


def other_chips(sent):
    n = lax.axis_size("row")
    return [shift(sent, "row", 2 * s) for s in range(1, n // 2)]


def other_groups(x):
    return [shift(x, "dp", s) for s in range(1, lax.axis_size("dp"))]


def on_device(
    tokens, cotangent, gate_blocks, gate_index, up_blocks, up_index, down_blocks, down_index
):
    n_col = lax.axis_size("col")
    parts = 1
    chunks = n_col // parts
    core = lax.rem(lax.axis_index("row"), 2).astype(jnp.int32).reshape(1)
    feats = tokens.shape[1] // BLK
    units = FF // BLK // n_col
    width = units * BLK
    slots = gate_blocks.shape[2]
    group_rows = tokens.shape[0] * n_col
    scale = 1.0 / math.sqrt(group_rows * lax.axis_size("dp"))

    def gather(x):
        got = {0: x}
        for d in z_order(n_col):
            got[d] = shift(x, "col", d)
        return [
            jnp.concatenate([got[d] for d in range(p * chunks, (p + 1) * chunks)], axis=0)
            for p in range(parts)
        ]

    def scatter(cut):
        return [cut[0]] + [shift(cut[d], "col", -d) for d in z_order(n_col)]

    def far_pieces(pairs):
        pieces = []
        for s in range(lax.axis_size("dp") - 1):
            for far in pairs:
                pieces += [far[s], swap_cores(far[s])]
        return pieces

    gate_table, gate_count = slot_table(gate_index, feats, units)
    up_table, up_count = slot_table(up_index, feats, units)
    down_table, down_count = slot_table(down_index, units, feats)

    x_parts = gather(tokens)
    x_whole = jnp.concatenate(x_parts, axis=0)
    (w_gate,) = densify((gate_table,), (gate_blocks[0, 0],), feats, units)
    gate_mine, gate_other = project(core, x_whole, w_gate, False)
    gate_swapped = swap_cores(gate_other)
    gate_sent = pair_sum(gate_mine, gate_swapped)

    gate_got = other_chips(gate_sent)
    c_parts = gather(after(cotangent, x_whole))
    c_whole = jnp.concatenate(c_parts, axis=0)
    x_groups = [x_whole] + other_groups(x_whole)
    up_mine, up_other, w_up = project_blocks(
        core, x_whole, up_table, up_blocks[0, 0], feats, units, False, gate_sent
    )
    token = mark(*gate_got, c_whole, *x_groups[1:])
    up_swapped = swap_cores(up_other)
    up_sent = pair_sum(up_mine, up_swapped, token)

    up_got = other_chips(up_sent)
    c_groups = [c_whole] + other_groups(c_whole)
    back_mine, back_other, w_down = project_blocks(
        core, c_whole, down_table, down_blocks[0, 0], units, feats, True, up_sent
    )
    token = mark(*up_got, *c_groups[1:])
    back_swapped = swap_cores(back_other)
    back_sent = pair_sum(back_mine, back_swapped, token)

    back_got = other_chips(back_sent)
    gate_sums = [gate_mine, gate_swapped] + gate_got
    up_sums = [up_mine, up_swapped] + up_got
    hidden = act(gate_sums, up_sums, back_sent)
    hidden_far = other_groups(hidden)
    hidden_pieces = [hidden, swap_cores(hidden)]
    out_cut = back(core, hidden_pieces, [w_down], n_col, False)
    by_gate, by_up = slopes(gate_sums, up_sums, out_cut[0])
    grads = act_grads([back_mine, back_swapped] + back_got, by_gate, by_up)
    hidden_pieces += far_pieces([[hold(far, grads) for far in hidden_far]])

    grads_far = other_groups(grads)
    grad_pieces = [grads, swap_cores(grads)]
    (down_grad,) = block_grads(
        core,
        (down_table,),
        (down_count,),
        hidden_pieces,
        c_groups,
        slots,
        scale,
        grads,
    )
    in_cut = back(core, grad_pieces, [w_gate, w_up], n_col, True, down_grad)
    out_kept = scatter(out_cut)
    (output,) = sum_chunks([out_kept], in_cut[0])
    grads_far = [hold(far, output) for far in grads_far]
    gate_grad, up_grad = block_grads(
        core,
        (gate_table, up_table),
        (gate_count, up_count),
        x_groups,
        grad_pieces + far_pieces([grads_far]),
        slots,
        scale,
    )
    (input_grad,) = sum_chunks([scatter(in_cut)], gate_grad)
    shape = gate_blocks.shape
    return (
        output,
        input_grad,
        gate_grad.reshape(shape),
        up_grad.reshape(shape),
        down_grad.reshape(shape),
    )


def solution(mesh):
    return jax.shard_map(
        on_device,
        mesh=mesh,
        in_specs=(
            P(("dp", "col"), "row"),
            P(("dp", "col"), "row"),
            P("row", "col", None, None, None),
            P("row", "col", None, None),
            P("row", "col", None, None, None),
            P("row", "col", None, None),
            P("row", "col", None, None, None),
            P("row", "col", None, None),
        ),
        out_specs=(
            P(("dp", "col"), "row"),
            P(("dp", "col"), "row"),
            P("row", "col", None, None, None),
            P("row", "col", None, None, None),
            P("row", "col", None, None, None),
        ),
        check_vma=False,
    )
```
